256 devices in a mesh: dp: 128 (over z, x, y), mp: 2 (over core).
Axes of the slice: x: 4, y: 4, z: 8, core: 2. Of those that a mesh axis runs over, the one named last changes fastest.
Arguments:
- points: bfloat16 [65536, 512], P('dp'), may hold values from -24 to 24
- patch_of: int32 [65536, 1], P('dp'), may hold values from 0 to 127; in each aligned block of 512 rows (0 to 511, 512 to 1023, ...) at most 8 rows name the same one
- qkv_weight: bfloat16 [512, 3, 512], P(None, None, 'mp'), may hold values from -10 to 10
- proj_weight: bfloat16 [512, 512], P('mp'), may hold values from -0.25 to 0.25
- fc1_weight: bfloat16 [512, 2048], P(None, 'mp'), may hold values from -0.25 to 0.25
- fc2_weight: bfloat16 [2048, 512], P('mp'), may hold values from -0.125 to 0.125
- cotangent: bfloat16 [65536, 512], P('dp'), may hold values from -24 to 24
Outputs:
- block_out: bfloat16 [65536, 512], P('dp')
- grad_qkv: float32 [512, 3, 512], P('dp', None, 'mp')
- grad_proj: float32 [512, 512], P('mp', 'dp')
- grad_fc1: float32 [512, 2048], P('dp', 'mp')
- grad_fc2: float32 [2048, 512], P('mp', 'dp')
The draws below stay inside these ranges and needn't reach their ends.
Inputs may be any that keep to these rules, and one draw needn't show every extreme that they name: `patch_of`: in each aligned block of 512 rows (the rows of one device) no patch is named by more than 8 rows, a bound that some block reaches; every patch is named by some row, so a patch holds 1 to 1024 points.
All inputs are finite; a program needn't handle non-finite values.
Results may differ from the reference program's by a relative error of at most 0.035.
The reference program's roundings to bfloat16 on the way count: a program that leaves them out, or rounds other values in their place, can miss the bound.
Values may be sent and summed in bfloat16 or wider, within the bound.
A program may use at most 128 MiB of HBM per device.

```python
import math
import jax
import jax.numpy as jnp
import numpy as np
from jax import lax

D = 512
HEAD_DIM = 16
FF = 2048
PATCH = 1024
PTS_DEV = 512
PATCHES = 128
MOST = 8
TOKENS = 65536


def draw_qkv_weight(key, part):
    key = jax.random.fold_in(key, 11)
    first = jax.random.fold_in(key, 0)
    spread = D ** (-0.5)
    return (jnp.clip(jax.random.normal(first, (D, 3, D), jnp.float32), -6.0, 6.0) * spread).astype(jnp.bfloat16)


def spiked(array, stream_key, source, target, blocks, factor):
    owner, partner = [(jnp.arange(array.shape[axis_at]) // (array.shape[axis_at] // blocks)).reshape([-1 if axis == axis_at else 1 for axis in range(array.ndim)]) for axis_at in (source, target)]
    chosen = jax.random.permutation(stream_key, blocks)[partner]
    strong = (owner == chosen) | (owner == (partner + blocks // 2) % blocks)
    return jnp.where(strong, factor * array, array)


def block_levels(stream_key, extent, shards, smallest, high):
    def one(position, parts):
        draws = jax.random.uniform(jax.random.fold_in(jax.random.fold_in(stream_key, 6), position), (parts,), jnp.float32, smallest / len(shards), high / len(shards))
        return jnp.repeat(jnp.exp(draws), extent[position] // parts).reshape((-1,) + (1,) * (len(extent) - position - 1))

    loudness = one(*shards[0])
    for cut in shards[1:]:
        loudness = loudness * one(*cut)
    return loudness


def assign_block(rng, own, number, rows, count, top, reach, lean):
    sequence = jax.random.permutation(rng, count)
    crowded, common = portions_of(count, rows * top, reach, lean, True), portions_of(count, rows * top, reach, lean, False)
    places = jnp.arange(count)

    def named(sizes, rotation):
        used = int((sizes > 0).sum())
        fixed = max(1, used // 4)
        passed = fixed + (places - fixed + rotation * (used - fixed)) % max(1, count - fixed)
        return jnp.zeros((count,), jnp.int32).at[sequence[jnp.where(places < fixed, places, passed)]].set(jnp.asarray(sizes, jnp.int32))

    sizes = jnp.where(number % 4 == 0, named(crowded, number // 4), named(common, number - number // 4 - 1))
    mixed = jax.random.permutation(jax.random.fold_in(own, 3), count)
    source_of, receiver = mixed[0:count // 2 * 2:2], mixed[1:count // 2 * 2:2]
    slack = jnp.minimum(sizes[source_of] - 1, reach - sizes[receiver]) // 2
    slack = jnp.where((source_of == sequence[0]) | (receiver == sequence[0]) | (sizes[receiver] == 0), 0, jnp.maximum(slack, 0))
    passed = jax.random.randint(jax.random.fold_in(own, 4), (count // 2,), 0, 1 << 20) % (slack + 1)
    sizes = sizes.at[source_of].add(-passed).at[receiver].add(passed)
    labels = jnp.searchsorted(jnp.cumsum(sizes), jnp.arange(rows * top), side="right").astype(jnp.int32)
    table = labels.reshape(top, rows).T
    table = table[jax.random.permutation(jax.random.fold_in(own, 1), rows)]
    rotation = jax.random.randint(jax.random.fold_in(own, 2), (rows, 1), 0, top)
    return jnp.take_along_axis(table, (jnp.arange(top)[None, :] + rotation) % top, axis=1)


def portions_of(number_of, total, reach, slope, full):
    weights = [(1 << 20) // math.isqrt(rank ** slope) + 1 for rank in range(1, number_of + 1)]
    largest = reach if full else min(reach, max(-(-total // number_of), total * weights[0] // sum(weights)))
    least = 1 if total - largest >= number_of - 1 else 0
    holding, surplus = [largest] + [least] * (number_of - 1), total - largest - least * (number_of - 1)
    while surplus > 0:
        free = [i for i in range(1, number_of) if holding[i] < largest] or [i for i in range(1, number_of) if holding[i] < reach]
        mass, budget = sum([weights[i] for i in free]), surplus
        for i in free:
            more = min(reach - holding[i], max(1, budget * weights[i] // mass), surplus)
            holding[i] = holding[i] + more
            surplus = surplus - more
    return np.array(holding)


def centred(rng, shape, deviation, bound, shards=(), held_as=jnp.bfloat16):
    entries = deviation * jax.random.normal(rng, shape, jnp.float32)
    if shards:
        entries = entries * block_levels(rng, shape, shards, -0.22, 0.18)
    return jnp.clip(entries, -bound, bound).astype(held_as)


def heavy_noise(own_key, extent, scale, most, cuts, heavy, held_as=jnp.bfloat16):
    values = scale * jax.random.normal(own_key, extent, jnp.float32)
    if cuts:
        values = values * block_levels(own_key, extent, cuts, -0.22, 0.18)
    return jnp.clip(spiked(values, jax.random.fold_in(own_key, 3), *heavy), -most, most).astype(held_as)


def setup_inputs(seed: int = 0) -> dict:
    streams_of = jax.random.split(jax.random.key(seed), 8)
    points = heavy_noise(streams_of[0], (TOKENS, D), 1.0, 24.0, ((0, 128),), (0, 1, 128, 5.5))
    patch_of_keys = jax.random.split(jax.random.fold_in(streams_of[1], 1), TOKENS // PTS_DEV)
    patch_of_turns = jax.random.permutation(jax.random.fold_in(streams_of[1], 3), TOKENS // PTS_DEV)
    patch_of = jax.vmap(lambda own, number: assign_block(jax.random.fold_in(streams_of[1], 2), own, number, PTS_DEV, PATCHES, 1, MOST, 2))(patch_of_keys, patch_of_turns).reshape((TOKENS, 1))
    qkv_weight = draw_qkv_weight(jax.random.fold_in(streams_of[7], 71), 0)
    proj_weight = centred(streams_of[3], (D, D), D ** -0.5, 0.25, ((0, 2),))
    fc1_weight = centred(streams_of[4], (D, FF), D ** -0.5, 0.25, ((1, 2),))
    fc2_weight = centred(streams_of[5], (FF, D), FF ** -0.5, 0.125, ((0, 2),))
    cotangent = heavy_noise(streams_of[6], (TOKENS, D), 1.0, 24.0, ((0, 128),), (0, 1, 128, 5.5))
    return {"points": points, "patch_of": patch_of, "qkv_weight": qkv_weight, "proj_weight": proj_weight, "fc1_weight": fc1_weight, "fc2_weight": fc2_weight, "cotangent": cotangent}


EPS = 1e-05
GELU_C = math.sqrt(2.0 / math.pi)

def widen(tensor):
    return lax.optimization_barrier(tensor).astype(jnp.float32)

def normalize(values):
    center = values - lax.optimization_barrier(jnp.mean(values, axis=-1, keepdims=True))
    inverse = lax.rsqrt(lax.optimization_barrier(jnp.mean(center * center, axis=-1, keepdims=True)) + EPS)
    return (center * inverse, inverse)

def normalize_back(normed, inverse, upstream):
    mean_grad = lax.optimization_barrier(jnp.mean(upstream, axis=-1, keepdims=True))
    mean_mixed = lax.optimization_barrier(jnp.mean(upstream * normed, axis=-1, keepdims=True))
    return inverse * (upstream - mean_grad - normed * mean_mixed)

def gelu_both(values):
    cubed_input = values * values * values
    tangent = jnp.tanh(GELU_C * (values + 0.044715 * cubed_input))
    output = 0.5 * values * (1.0 + tangent)
    derivative = 0.5 * (1.0 + tangent) + 0.5 * values * (1.0 - tangent * tangent) * GELU_C * (1.0 + 3.0 * 0.044715 * values * values)
    return (output, derivative)

def grouped(tensor):
    length = tensor.shape[0]
    blocks = tensor.shape[1] // (4 * HEAD_DIM)
    return tensor.reshape(length, blocks, 4, HEAD_DIM).transpose(1, 0, 2, 3)

def ungrouped(tensor):
    blocks, length = (tensor.shape[0], tensor.shape[1])
    return tensor.transpose(1, 0, 2, 3).reshape(length, blocks * 4 * HEAD_DIM)

def head_scores(queries, keys, occupied):
    scores = jnp.einsum('qhd,khd->hqk', queries.astype(jnp.float32), keys.astype(jnp.float32)) * HEAD_DIM ** (-0.5)
    return jnp.where(occupied[None, None, :], scores, -1e+30)

def attend(queries, keys, values, occupied):

    def one_group(operands):
        group_query, group_key, group_value = operands
        scores = head_scores(group_query, group_key, occupied)
        maxima = lax.optimization_barrier(jnp.max(scores, axis=2, keepdims=True))
        exponent = jnp.exp(scores - maxima)
        totals = lax.optimization_barrier(jnp.sum(exponent, axis=2, keepdims=True))
        weights = jnp.exp(scores - maxima) / totals
        result = jnp.einsum('hqk,khd->qhd', widen(weights.astype(jnp.bfloat16)), group_value.astype(jnp.float32))
        return (result.astype(jnp.bfloat16), maxima, totals)
    outputs, maxima, totals = lax.map(one_group, (grouped(queries), grouped(keys), grouped(values)))
    return (ungrouped(outputs), maxima, totals)

def attend_back(queries, keys, values, occupied, attended, d_attended, maxima, totals):

    def one_group(operands):
        group_query, group_key, group_value, group_out, group_grad, group_max, group_total = operands
        scores = head_scores(group_query, group_key, occupied)
        weights = jnp.exp(scores - group_max) / group_total
        rounded = widen(weights.astype(jnp.bfloat16))
        grad_wide = group_grad.astype(jnp.float32)
        d_weights = jnp.einsum('qhd,khd->hqk', grad_wide, group_value.astype(jnp.float32))
        delta = jnp.einsum('qhd,qhd->hq', grad_wide, group_out.astype(jnp.float32))
        d_scores = widen((weights * (d_weights - delta[:, :, None]) * HEAD_DIM ** (-0.5)).astype(jnp.bfloat16))
        grad_query = jnp.einsum('hqk,khd->qhd', d_scores, group_key.astype(jnp.float32)).astype(jnp.bfloat16)
        grad_key = jnp.einsum('hqk,qhd->khd', d_scores, group_query.astype(jnp.float32)).astype(jnp.bfloat16)
        grad_value = jnp.einsum('hqk,qhd->khd', rounded, grad_wide).astype(jnp.bfloat16)
        return (grad_query, grad_key, grad_value)
    results = lax.map(one_group, (grouped(queries), grouped(keys), grouped(values), grouped(attended), grouped(d_attended), maxima, totals))
    return (ungrouped(results[0]), ungrouped(results[1]), ungrouped(results[2]))

def patch_pass(rows_in, upstream, occupied, qkv_weight, proj_weight, fc1_weight, fc2_weight):
    wide_in = rows_in.astype(jnp.float32)
    normed_one, inverse_one = normalize(wide_in)
    normed_in = normed_one.astype(jnp.bfloat16)
    projected = jnp.einsum('rd,dje->jre', widen(normed_in), qkv_weight.astype(jnp.float32)).astype(jnp.bfloat16)
    attended, maxima, totals = attend(projected[0], projected[1], projected[2], occupied)
    mixed = wide_in + jnp.dot(attended, proj_weight, preferred_element_type=jnp.float32)
    normed_two, inverse_two = normalize(mixed)
    normed_mid = normed_two.astype(jnp.bfloat16)
    pre_act = jnp.dot(normed_mid, fc1_weight, preferred_element_type=jnp.float32)
    activation, derivative = gelu_both(pre_act)
    act_low = activation.astype(jnp.bfloat16)
    block_rows = (mixed + jnp.dot(act_low, fc2_weight, preferred_element_type=jnp.float32)).astype(jnp.bfloat16)
    grad_fc2 = jnp.dot(act_low.T, upstream, preferred_element_type=jnp.float32)
    d_pre = (jnp.dot(upstream, fc2_weight.T, preferred_element_type=jnp.float32) * derivative).astype(jnp.bfloat16)
    grad_fc1 = jnp.dot(normed_mid.T, d_pre, preferred_element_type=jnp.float32)
    back_norm = jnp.dot(d_pre, fc1_weight.T, preferred_element_type=jnp.float32)
    d_mixed = (upstream.astype(jnp.float32) + normalize_back(normed_two, inverse_two, back_norm)).astype(jnp.bfloat16)
    grad_proj = jnp.dot(attended.T, d_mixed, preferred_element_type=jnp.float32)
    d_attended = jnp.dot(d_mixed, proj_weight.T, preferred_element_type=jnp.float32).astype(jnp.bfloat16)
    grad_query, grad_key, grad_value = attend_back(projected[0], projected[1], projected[2], occupied, attended, d_attended, maxima, totals)
    stacked = jnp.stack([grad_query, grad_key, grad_value])
    grad_qkv = jnp.einsum('rd,jre->dje', widen(normed_in), widen(stacked))
    return (block_rows, (grad_qkv, grad_proj, grad_fc1, grad_fc2))

def reference(points, patch_of, qkv_weight, proj_weight, fc1_weight, fc2_weight, cotangent):
    target = patch_of[:, 0].astype(jnp.int32)
    order = jnp.argsort(target, stable=True).astype(jnp.int32)
    sorted_target = target[order]
    counts = jax.ops.segment_sum(jnp.ones_like(target), target, num_segments=PATCHES).astype(jnp.int32)
    starts = (jnp.cumsum(counts) - counts).astype(jnp.int32)
    within = jnp.arange(TOKENS, dtype=jnp.int32) - starts[sorted_target]
    placement = jnp.zeros((TOKENS,), jnp.int32).at[order].set((sorted_target * PATCH + within).astype(jnp.int32))
    point_rows = jnp.zeros((PATCHES * PATCH, D), jnp.bfloat16).at[placement].set(points).reshape(PATCHES, PATCH, D)
    upstream_rows = jnp.zeros((PATCHES * PATCH, D), jnp.bfloat16).at[placement].set(cotangent).reshape(PATCHES, PATCH, D)
    occupied = jnp.zeros((PATCHES * PATCH,), jnp.bool_).at[placement].set(True).reshape(PATCHES, PATCH)

    def one_patch(carry, operands):
        block_rows, grads = patch_pass(operands[0], operands[1], operands[2], qkv_weight, proj_weight, fc1_weight, fc2_weight)
        return (jax.tree.map(jnp.add, carry, grads), block_rows)
    start_grads = (jnp.zeros((D, 3, D), jnp.float32), jnp.zeros((D, D), jnp.float32), jnp.zeros((D, FF), jnp.float32), jnp.zeros((FF, D), jnp.float32))
    grads, outputs = lax.scan(one_patch, start_grads, (point_rows, upstream_rows, occupied))
    block_out = outputs.reshape(PATCHES * PATCH, D)[placement]
    return (block_out, grads[0], grads[1], grads[2], grads[3])
```

```python
import functools
import math

import jax
import jax.numpy as jnp
from jax import lax
from jax.experimental import pallas as pl
from jax.experimental.pallas import tpu as pltpu
from jax.sharding import PartitionSpec as P

MESH = pl.DeviceIdType.MESH
F32 = jnp.float32
BF16 = jnp.bfloat16
VMEM = pl.BlockSpec(memory_space=pltpu.VMEM)

HEADS = 16
HEAD_DIM = 16
PATCH = 1024
ROWS = 512
D = 512
FF = 1024
EPS = 1e-05
GELU_C = math.sqrt(2.0 / math.pi)
EXP2_SCALE = HEAD_DIM**-0.5 * math.log2(math.e)
EMPTY = 64.0
MASKED = -1e30
NX, NY, NZ = 4, 4, 8
PAIRS = 64
GW = 2304
QW = 768


def dot(left, right, dims):
    return lax.dot_general(left, right, (dims, ((), ())), preferred_element_type=F32)


NN = ((1,), (0,))
NT = ((1,), (1,))
TN = ((0,), (0,))


def params(**more):
    return pltpu.CompilerParams(vmem_limit_bytes=56 << 20, **more)


def normalize(values):
    center = values - jnp.mean(values, axis=-1, keepdims=True)
    inverse = lax.rsqrt(jnp.mean(center * center, axis=-1, keepdims=True) + EPS)
    return center * inverse, inverse


def split3(x):
    a = x.astype(BF16)
    r = x - a.astype(F32)
    b = r.astype(BF16)
    return a, b, (r - b.astype(F32)).astype(BF16)


def pack(rows):
    n = rows.shape[0] // 8
    pieces = rows.reshape(n, 8, D)
    return jnp.concatenate([pieces[:, :, : D // 2], pieces[:, :, D // 2 :]], axis=1).astype(BF16)


def unpack(pieces):
    wide = pieces.astype(F32)
    n = wide.shape[0]
    return jnp.concatenate([wide[:, :8], wide[:, 8:]], axis=2).reshape(8 * n, D)


def pair_barrier(me, core, extra=()):
    barrier = pltpu.get_barrier_semaphore()
    parity = lax.rem(core + me, 2)

    def greet(i, carry):
        other = 2 * lax.rem(lax.div(me, 2) + i, PAIRS) + parity
        pl.semaphore_signal(barrier, inc=1, device_id=(other, core), device_id_type=MESH)
        return carry

    lax.fori_loop(1, PAIRS, greet, 0)

    @pl.when(core == 1)
    def _():
        other = 2 * lax.div(me, 2) + parity
        pl.semaphore_signal(barrier, inc=1, device_id=(other, core), device_id_type=MESH)

    pl.semaphore_signal(barrier, inc=1, device_id=(me, 1 - core), device_id_type=MESH)
    for other in extra:
        pl.semaphore_signal(barrier, inc=1, device_id=(other, core), device_id_type=MESH)
    pl.semaphore_wait(barrier, PAIRS + core + len(extra))


def pair_sends(me, core, out, landing, send_sem, recv_sem):
    parity = lax.rem(core + me, 2)
    mine = lax.div(me, 2)

    def push(place):
        pltpu.make_async_remote_copy(
            src_ref=out.at[place],
            dst_ref=landing.at[core, mine],
            send_sem=send_sem,
            recv_sem=recv_sem,
            device_id=(2 * place + parity, core),
            device_id_type=MESH,
        ).start()

    @pl.when(core == 0)
    def _():
        pltpu.make_async_copy(out.at[mine], landing.at[core, mine], recv_sem).start()

    @pl.when(core == 1)
    def _():
        push(mine)

    def step(i, carry):
        push(lax.rem(mine + i, PAIRS))
        return carry

    lax.fori_loop(1, PAIRS, step, 0)


def pair_arrived(core, landing, recv_sem):
    pltpu.make_async_copy(landing.at[core], landing.at[core], recv_sem).wait()


def pair_sent(core, out, send_sem):
    most = out.at[pl.ds(0, PAIRS - 1)]
    pltpu.make_async_copy(most, most, send_sem).wait()

    @pl.when(core == 1)
    def _():
        pltpu.make_async_copy(out.at[0], out.at[0], send_sem).wait()


def to_sibling(me, core, landing, send_sem, recv_sem):
    return pltpu.make_async_remote_copy(
        src_ref=landing.at[core],
        dst_ref=landing.at[core],
        send_sem=send_sem,
        recv_sem=recv_sem,
        device_id=(me, 1 - core),
        device_id_type=MESH,
    )


def sibling_arrived(core, landing, recv_sem):
    pltpu.make_async_copy(landing.at[1 - core], landing.at[1 - core], recv_sem).wait()


def slot_rows(patch, me):
    member = (lax.broadcasted_iota(jnp.int32, (128, ROWS), 0) == patch).astype(BF16)
    before = (
        lax.broadcasted_iota(jnp.int32, (ROWS, ROWS), 0)
        < lax.broadcasted_iota(jnp.int32, (ROWS, ROWS), 1)
    ).astype(BF16)
    earlier = dot(member, before, NN)
    within = jnp.sum(earlier * member.astype(F32), axis=0, keepdims=True).astype(jnp.int32)
    return ((patch + me) & 1) * (PATCH // 2) + (patch >> 1) * 8 + within


def dispatch_kernel(
    points, cotangent, patch, rows_out, upstream_out, bias_out, slot_out,
    out_p, out_c, land_p, land_c, send_sem, recv_sem,
):
    me, core = lax.axis_index("dp"), lax.axis_index("mp")
    slot = slot_rows(patch[...], me)
    slot_out[...] = jnp.broadcast_to(slot, (8, ROWS))
    place = lax.broadcasted_iota(jnp.int32, (PATCH // 2, ROWS), 0) + core * (PATCH // 2)
    chosen = (place == slot).astype(BF16)
    filled = dot(chosen, jnp.ones((ROWS, 128), BF16), NN)
    fill = EMPTY * (1.0 - jnp.concatenate([filled] * (D // 128), axis=1))
    out_p[...] = pack(dot(chosen, points[...], NN) + fill)
    pair_barrier(me, core)
    pair_sends(me, core, out_p, land_p, send_sem.at[0], recv_sem.at[0])
    out_c[...] = pack(dot(chosen, cotangent[...], NN))
    pair_sends(me, core, out_c, land_c, send_sem.at[1], recv_sem.at[1])
    pair_arrived(core, land_p, recv_sem.at[0])
    first = to_sibling(me, core, land_p, send_sem.at[2], recv_sem.at[2])
    first.start()
    pair_arrived(core, land_c, recv_sem.at[1])
    second = to_sibling(me, core, land_c, send_sem.at[3], recv_sem.at[3])
    second.start()
    sibling_arrived(core, land_p, recv_sem.at[2])
    ones = jnp.ones((16, 128), BF16)
    for half in range(2):
        for part in range(2):
            pieces = slice(part * 32, part * 32 + 32)
            at = half * 512 + part * 256
            wide = unpack(land_p[half, pieces])
            empty = wide > 0.5 * EMPTY
            rows_out[at : at + 256, :] = jnp.where(empty, 0.0, wide).astype(BF16)
            count = dot(ones, jnp.where(empty[:, :128], 1.0, 0.0).astype(BF16), NT)
            first_row = lax.broadcasted_iota(jnp.int32, (16, 256), 0) == 0
            bias_out[:, at : at + 256] = jnp.where(
                first_row & (count > 0.5), MASKED, 0.0
            ).astype(BF16)
    sibling_arrived(core, land_c, recv_sem.at[3])
    for half in range(2):
        for part in range(2):
            pieces = slice(part * 32, part * 32 + 32)
            at = half * 512 + part * 256
            upstream_out[at : at + 256, :] = unpack(land_c[half, pieces]).astype(BF16)
    first.wait_send()
    second.wait_send()
    pair_sent(core, out_p, send_sem.at[0])
    pair_sent(core, out_c, send_sem.at[1])


def dispatch(points, cotangent, patch):
    pieces = pltpu.VMEM((PAIRS, 16, D // 2), BF16)
    landing = pltpu.VMEM((2, PAIRS, 16, D // 2), BF16)
    return pl.pallas_call(
        dispatch_kernel,
        out_shape=(
            jax.ShapeDtypeStruct((PATCH, D), BF16),
            jax.ShapeDtypeStruct((PATCH, D), BF16),
            jax.ShapeDtypeStruct((16, PATCH), BF16),
            jax.ShapeDtypeStruct((8, ROWS), jnp.int32),
        ),
        in_specs=[VMEM] * 3,
        out_specs=(VMEM,) * 4,
        scratch_shapes=[
            pieces,
            pieces,
            landing,
            landing,
            pltpu.SemaphoreType.DMA((4,)),
            pltpu.SemaphoreType.DMA((4,)),
        ],
        compiler_params=params(collective_id=1, has_side_effects=True),
        name="dispatch",
    )(points, cotangent, patch)


def forward_head(query, key, value, bias):
    scaled = split3(query.astype(F32) * EXP2_SCALE)
    wide_query = jnp.concatenate([*scaled, jnp.ones((16, PATCH), BF16)], axis=0)
    wide_key = jnp.concatenate([key, key, key, bias], axis=0)
    scores = dot(wide_key, wide_query, TN)
    maxima = jnp.max(scores, axis=0, keepdims=True)
    weights = jnp.exp2(scores - maxima)
    totals = jnp.sum(weights, axis=0, keepdims=True)
    result = dot(value, weights.astype(BF16), NN) / totals
    return result.astype(BF16), maxima + jnp.log2(totals)


def attend_kernel(rows, weight, bias, normed_out, qkv_out, attended_out, lse_out):
    for part in range(4):
        at = slice(part * 256, part * 256 + 256)
        normed, _ = normalize(rows[at, :].astype(F32))
        normed_out[at, :] = normed.astype(BF16)
    for j in range(3):
        projected = dot(weight[j * 256 : j * 256 + 256, :], normed_out[...], NT)
        qkv_out[j] = projected.astype(BF16).reshape(HEADS, HEAD_DIM, PATCH)
    mask = bias[...]

    def pair(i, carry):
        for u in range(2):
            h = 2 * i + u
            result, lse = forward_head(qkv_out[0, h], qkv_out[1, h], qkv_out[2, h], mask)
            attended_out[h] = result
            lse_out[h] = jnp.broadcast_to(lse, (8, PATCH))
        return carry

    lax.fori_loop(0, HEADS // 2, pair, 0)


def attend(rows, weight, bias):
    heads = (HEADS, HEAD_DIM, PATCH)
    return pl.pallas_call(
        attend_kernel,
        out_shape=(
            jax.ShapeDtypeStruct((PATCH, D), BF16),
            jax.ShapeDtypeStruct((3, *heads), BF16),
            jax.ShapeDtypeStruct(heads, BF16),
            jax.ShapeDtypeStruct((HEADS, 8, PATCH), F32),
        ),
        in_specs=[VMEM] * 3,
        out_specs=(VMEM,) * 4,
        compiler_params=params(),
        name="attend",
    )(rows, weight, bias)


def backward_head(query, key, value, bias, attended, upstream, lse):
    shape = (16, PATCH)
    row = lax.broadcasted_iota(jnp.int32, shape, 0)
    one = jnp.ones(shape, BF16)
    zero = jnp.zeros(shape, BF16)

    def stacked(*given):
        total = zero
        for at, value_at in enumerate(given):
            total = jnp.where(row == at, value_at, total)
        return total

    lse_pieces = split3(-jnp.broadcast_to(lse, shape))
    scaled = split3(query.astype(F32) * EXP2_SCALE)
    wide_query = jnp.concatenate([*scaled, stacked(one, *lse_pieces)], axis=0)
    wide_key = jnp.concatenate([key, key, key, stacked(bias, one, one, one)], axis=0)
    scale = HEAD_DIM**-0.5
    upstream_wide = upstream.astype(F32)
    delta = -scale * jnp.sum(upstream_wide * attended.astype(F32), axis=0, keepdims=True)
    delta_pieces = split3(jnp.broadcast_to(delta, shape))
    wide_upstream = jnp.concatenate(
        [(scale * upstream_wide).astype(BF16), stacked(*delta_pieces)], axis=0
    )
    wide_value = jnp.concatenate([value, stacked(one, one, one)], axis=0)
    d_query, d_key, d_value = [], None, None
    for part in range(2):
        at = slice(part * 512, part * 512 + 512)
        weights = jnp.exp2(dot(wide_key, wide_query[:, at], TN))
        d_scores = (weights * dot(wide_value, wide_upstream[:, at], TN)).astype(BF16)
        d_query.append(dot(key, d_scores, NN))
        more_key = dot(query[:, at], d_scores, NT)
        more_value = dot(upstream[:, at], weights.astype(BF16), NT)
        d_key = more_key if d_key is None else d_key + more_key
        d_value = more_value if d_value is None else d_value + more_value
    return jnp.concatenate(d_query, axis=1).astype(BF16), d_key.astype(BF16), d_value.astype(BF16)


def attend_back_kernel(normed, qkv, bias, attended, upstream, lse, grad_out, d_qkv):
    mask = bias[...]

    def one_head(h, carry):
        d_query, d_key, d_value = backward_head(
            qkv[0, h], qkv[1, h], qkv[2, h], mask, attended[h], upstream[h], lse[h][0:1]
        )
        d_qkv[0, h] = d_query
        d_qkv[1, h] = d_key
        d_qkv[2, h] = d_value
        return carry

    lax.fori_loop(0, HEADS, one_head, 0)
    for j in range(3):
        grad = dot(d_qkv[j].reshape(256, PATCH), normed[...], NN)
        grad_out[:, j * 256 : j * 256 + 256] = grad.T.astype(BF16)


def attend_back(normed, qkv, bias, attended, upstream, lse):
    return pl.pallas_call(
        attend_back_kernel,
        out_shape=jax.ShapeDtypeStruct((D, QW), BF16),
        in_specs=[VMEM] * 6,
        out_specs=VMEM,
        scratch_shapes=[pltpu.VMEM((3, HEADS, HEAD_DIM, PATCH), BF16)],
        compiler_params=params(),
        name="attend_back",
    )(normed, qkv, bias, attended, upstream, lse)


def gelu_both(values):
    squared = values * values
    tangent = jnp.tanh(GELU_C * (values + 0.044715 * squared * values))
    half = 0.5 * (1.0 + tangent)
    derivative = half + 0.5 * values * (1.0 - tangent * tangent) * GELU_C * (
        1.0 + 3.0 * 0.044715 * squared
    )
    return values * half, derivative


CHUNK = 256


def feed_forward_kernel(
    attended, rows, upstream, proj, fc1, fc2, block_out, grad_out, d_attended_out,
    snd1, rcv1, snd2, rcv2, snd3, rcv3, own2, mixed, normed_mid, inverse, act, d_pre, d_mixed,
    send_sem, recv_sem,
):
    me, core = lax.axis_index("dp"), lax.axis_index("mp")
    sibling = (me, 1 - core)
    barrier = pltpu.get_barrier_semaphore()
    pl.semaphore_signal(barrier, inc=1, device_id=sibling, device_id_type=MESH)
    chunks = PATCH // CHUNK

    def place(i):
        return lax.rem(i + 2 * (1 - core), chunks)

    def span(k):
        return pl.ds(pl.multiple_of(k * CHUNK, CHUNK), CHUNK)

    def copy(kind, i, src, dst):
        return pltpu.make_async_remote_copy(
            src_ref=src,
            dst_ref=dst,
            send_sem=send_sem.at[kind, i],
            recv_sem=recv_sem.at[kind, i],
            device_id=sibling,
            device_id_type=MESH,
        )

    def copy1(k):
        return copy(0, k, snd1.at[span(k), :], rcv1.at[span(k), :])

    def copy2(i):
        at = pl.ds(i * CHUNK, CHUNK)
        return copy(1, i, snd2.at[at, :], rcv2.at[at, :])

    def copy3(k):
        return copy(2, k, snd3.at[span(k), :], rcv3.at[span(k), :])

    for k in range(chunks):
        partial = dot(attended[:, k * CHUNK : (k + 1) * CHUNK], proj[...], TN)
        snd1[k * CHUNK : (k + 1) * CHUNK, :] = partial.astype(BF16)
        if k == 0:
            pl.semaphore_wait(barrier, 1)
        copy1(k).start()

    for i in range(chunks):
        k = place(i)
        at = span(k)
        copy1(k).wait_recv()
        total = rows[at, :].astype(F32) + (snd1[at, :].astype(F32) + rcv1[at, :].astype(F32))
        mixed[at, :] = total
        normed, inv = normalize(total)
        inverse[at, :] = jnp.broadcast_to(inv, (CHUNK, 128))
        low = normed.astype(BF16)
        normed_mid[at, :] = low
        activation, derivative = gelu_both(dot(low, fc1[...], NN))
        act_low = activation.astype(BF16)
        act[at, :] = act_low
        partial = dot(act_low, fc2[...], NN).astype(BF16)
        if i < 2:
            snd2[i * CHUNK : (i + 1) * CHUNK, :] = partial
            copy2(i).start()
        else:
            own2[(i - 2) * CHUNK : (i - 1) * CHUNK, :] = partial
        d_low = (dot(upstream[at, :], fc2[...], NT) * derivative).astype(BF16)
        d_pre[at, :] = d_low
        snd3[at, :] = dot(d_low, fc1[...], NT).astype(BF16)
        copy3(k).start()

    for part in range(4):
        cols = slice(part * 256, part * 256 + 256)
        grad_out[:, cols] = dot(normed_mid[...], d_pre[:, cols], TN).astype(BF16)
        grad_out[:, 1024 + part * 256 : 1280 + part * 256] = dot(
            upstream[...], act[:, cols], TN
        ).astype(BF16)

    for i in range(chunks):
        k = place(i)
        at = span(k)
        copy3(k).wait_recv()
        back = snd3[at, :].astype(F32) + rcv3[at, :].astype(F32)
        inv = inverse[at, :][:, 0:1]
        total = mixed[at, :]
        center = total - jnp.mean(total, axis=-1, keepdims=True)
        normed = center * inv
        mean_grad = jnp.mean(back, axis=-1, keepdims=True)
        mean_mixed = jnp.mean(back * normed, axis=-1, keepdims=True)
        through = inv * (back - mean_grad - normed * mean_mixed)
        d_mixed[at, :] = (upstream[at, :].astype(F32) + through).astype(BF16)

    for k in range(chunks):
        at = slice(k * CHUNK, (k + 1) * CHUNK)
        d_attended_out[:, at] = dot(proj[...], d_mixed[at, :], NT).astype(BF16)
    grad_out[:, 2048:2304] = dot(attended[...], d_mixed[...], NN).T.astype(BF16)

    for i in range(2):
        copy2(i).wait_recv()
        own = slice(i * CHUNK, (i + 1) * CHUNK)
        total = mixed[span(place(i + 2)), :] + (own2[own, :].astype(F32) + rcv2[own, :].astype(F32))
        block_out[i * 32 : i * 32 + 32] = pack(total.astype(BF16).astype(F32))
    for k in range(chunks):
        copy1(k).wait_send()
        copy3(k).wait_send()
    for i in range(2):
        copy2(i).wait_send()


def feed_forward(attended, rows, upstream, proj, fc1, fc2):
    whole = pltpu.VMEM((PATCH, D), BF16)
    half = pltpu.VMEM((PATCH // 2, D), BF16)
    return pl.pallas_call(
        feed_forward_kernel,
        out_shape=(
            jax.ShapeDtypeStruct((PAIRS, 16, D // 2), BF16),
            jax.ShapeDtypeStruct((D, GW), BF16),
            jax.ShapeDtypeStruct((256, PATCH), BF16),
        ),
        in_specs=[VMEM] * 6,
        out_specs=(VMEM,) * 3,
        scratch_shapes=[
            whole,
            whole,
            half,
            half,
            whole,
            whole,
            half,
            pltpu.VMEM((PATCH, D), F32),
            whole,
            pltpu.VMEM((PATCH, 128), F32),
            pltpu.VMEM((PATCH, FF), BF16),
            pltpu.VMEM((PATCH, FF), BF16),
            whole,
            pltpu.SemaphoreType.DMA((3, 4)),
            pltpu.SemaphoreType.DMA((3, 4)),
        ],
        compiler_params=params(collective_id=2, has_side_effects=True),
        name="feed_forward",
    )(attended, rows, upstream, proj, fc1, fc2)


def axis_peers(me):
    z, x, y = lax.div(me, NX * NY), lax.rem(lax.div(me, NY), NX), lax.rem(me, NY)
    at_x = [(z * NX + lax.rem(x + d, NX)) * NY + y for d in range(NX)]
    at_z = [(lax.rem(z + d, NZ) * NX + x) * NY + y for d in range(NZ)]
    at_y = [(z * NX + x) * NY + lax.rem(y + d, NY) for d in range(NY)]
    return (z, x, y), (at_x, at_z, at_y)


class ReduceScatter:
    def __init__(self, me, core, grad, land, sems):
        self.core = core
        self.place, self.peers = axis_peers(me)
        self.grad, self.sems = grad, sems
        self.land_x, self.mid, self.land_z, self.low, self.land_y = land

    def copy(self, phase, d, src, dst):
        send, recv = self.sems
        base = (0, NX - 1, NX + NZ - 2)[phase]
        return pltpu.make_async_remote_copy(
            src_ref=src,
            dst_ref=dst,
            send_sem=send.at[base + d - 1],
            recv_sem=recv.at[base + d - 1],
            device_id=(self.peers[phase][d], self.core),
            device_id_type=MESH,
        )

    def copies(self, phase):
        z, x, _ = self.place
        if phase == 0:
            return [
                self.copy(0, d, self.grad.at[:, lax.rem(x + d, NX)], self.land_x.at[d - 1])
                for d in range(1, NX)
            ]
        if phase == 1:
            return [
                self.copy(1, d, self.mid.at[lax.rem(z + d, NZ)], self.land_z.at[d - 1])
                for d in range(1, NZ)
            ]
        return [self.copy(2, d, self.low, self.land_y.at[d - 1]) for d in range(1, NY)]

    def start(self, phase):
        for one in self.copies(phase):
            one.start()

    def arrived(self, phase):
        for one in self.copies(phase):
            one.wait_recv()

    def after_x(self):
        self.arrived(0)
        _, x, _ = self.place

        def step(i, carry):
            total = self.grad[i, x].astype(F32)
            for d in range(NX - 1):
                total = total + self.land_x[d, i].astype(F32)
            self.mid[i] = total.astype(BF16)
            return carry

        lax.fori_loop(0, NZ, step, 0)
        self.start(1)

    def after_z(self):
        self.arrived(1)
        z, _, _ = self.place
        total = self.mid[z].astype(F32)
        for d in range(NZ - 1):
            total = total + self.land_z[d].astype(F32)
        self.low[...] = total.astype(BF16)
        self.start(2)

    def after_y(self):
        self.arrived(2)
        _, _, y = self.place
        total = self.low[...].astype(F32)
        for d in range(NY - 1):
            total = total + self.land_y[d].astype(F32)
        result = total[0:4]
        for other in range(1, NY):
            result = jnp.where(y == other, total[4 * other : 4 * other + 4], result)
        return result

    def finish(self):
        for phase in range(3):
            for one in self.copies(phase):
                one.wait_send()


def reduce_scratch(columns):
    return [
        pltpu.VMEM((NX - 1, NZ, 16, columns), BF16),
        pltpu.VMEM((NZ, 16, columns), BF16),
        pltpu.VMEM((NZ - 1, 16, columns), BF16),
        pltpu.VMEM((16, columns), BF16),
        pltpu.VMEM((NY - 1, 16, columns), BF16),
        pltpu.SemaphoreType.DMA((NX + NY + NZ - 3,)),
        pltpu.SemaphoreType.DMA((NX + NY + NZ - 3,)),
    ]


def collect_kernel(block, slot, grad, grad_qkv, rows_out, sums_out, qkv_out, *scratch):
    me, core = lax.axis_index("dp"), lax.axis_index("mp")
    land, send_sem, recv_sem = scratch[:3]
    first = ReduceScatter(me, core, grad, scratch[3:8], scratch[8:10])
    second = ReduceScatter(me, core, grad_qkv, scratch[10:15], scratch[15:17])
    _, peers = axis_peers(me)
    pair_barrier(me, core, [p for axis in peers for p in axis[1:]])
    second.start(0)
    first.start(0)
    pair_sends(me, core, block, land, send_sem.at[0], recv_sem.at[0])
    second.after_x()
    first.after_x()
    second.after_z()
    first.after_z()
    pair_arrived(core, land, recv_sem.at[0])
    swap = to_sibling(me, core, land, send_sem.at[1], recv_sem.at[1])
    swap.start()
    qkv_out[...] = second.after_y()
    sums_out[...] = first.after_y()
    sibling_arrived(core, land, recv_sem.at[1])
    total = None
    for half in range(2):
        place = lax.broadcasted_iota(jnp.int32, (PATCH // 2, ROWS), 0) + half * (PATCH // 2)
        chosen = (place == slot[0:1, :]).astype(BF16)
        part = dot(chosen, unpack(land[half]).astype(BF16), TN)
        total = part if total is None else total + part
    rows_out[...] = total.astype(BF16)
    swap.wait_send()
    pair_sent(core, block, send_sem.at[0])
    first.finish()
    second.finish()


def collect(block, slot, grad, grad_qkv):
    return pl.pallas_call(
        collect_kernel,
        out_shape=(
            jax.ShapeDtypeStruct((ROWS, D), BF16),
            jax.ShapeDtypeStruct((4, GW), F32),
            jax.ShapeDtypeStruct((4, QW), F32),
        ),
        in_specs=[VMEM] * 4,
        out_specs=(VMEM,) * 3,
        scratch_shapes=[
            pltpu.VMEM((2, PAIRS, 16, D // 2), BF16),
            pltpu.SemaphoreType.DMA((2,)),
            pltpu.SemaphoreType.DMA((2,)),
            *reduce_scratch(GW),
            *reduce_scratch(QW),
        ],
        compiler_params=params(collective_id=3, has_side_effects=True),
        name="collect",
    )(block, slot, grad.reshape(NZ, NX, 16, GW), grad_qkv.reshape(NZ, NX, 16, QW))


def per_device(points, patch_of, qkv_weight, proj_weight, fc1_weight, fc2_weight, cotangent):
    weight = qkv_weight.reshape(D, QW).T
    rows, upstream, bias, slot = dispatch(points, cotangent, patch_of.reshape(1, ROWS))
    normed, qkv, attended, lse = attend(rows, weight, bias)
    block, grad, d_attended = feed_forward(
        attended.reshape(256, PATCH), rows, upstream, proj_weight, fc1_weight, fc2_weight
    )
    grad_qkv = attend_back(
        normed, qkv, bias, attended, d_attended.reshape(HEADS, HEAD_DIM, PATCH), lse
    )
    block_out, sums, qkv_sums = collect(block, slot, grad, grad_qkv)
    return (
        block_out,
        qkv_sums.reshape(4, 3, 256),
        sums[:, 2048:2304].T,
        sums[:, :1024],
        sums[:, 1024:2048].T,
    )


def solution(mesh):
    placed = (
        P("dp", None),
        P("dp", None),
        P(None, None, "mp"),
        P("mp", None),
        P(None, "mp"),
        P("mp", None),
        P("dp", None),
    )
    return jax.shard_map(
        per_device,
        mesh=mesh,
        in_specs=placed,
        out_specs=(P("dp", None), P("dp", None, "mp"), P("mp", "dp"), P("dp", "mp"), P("mp", "dp")),
        check_vma=False,
    )
```

```python
import functools
import math

import jax
import jax.numpy as jnp
from jax import lax
from jax.experimental import pallas as pl
from jax.experimental.pallas import tpu as pltpu
from jax.sharding import PartitionSpec as P

MESH = pl.DeviceIdType.MESH
F32 = jnp.float32
BF16 = jnp.bfloat16
VMEM = pl.BlockSpec(memory_space=pltpu.VMEM)

HEADS = 16
HEAD_DIM = 16
PATCH = 1024
ROWS = 512
D = 512
FF = 1024
EPS = 1e-05
GELU_C = math.sqrt(2.0 / math.pi)
EXP2_SCALE = HEAD_DIM**-0.5 * math.log2(math.e)
EMPTY = 64.0
MASKED = -1e30
NX, NY, NZ = 4, 4, 8
PAIRS = 64
FIRST_HEADS = 12
AW = 1280
BW = 1024
QA = 3 * HEAD_DIM * FIRST_HEADS
QB = 3 * HEAD_DIM * (HEADS - FIRST_HEADS)


def dot(left, right, dims):
    return lax.dot_general(left, right, (dims, ((), ())), preferred_element_type=F32)


NN = ((1,), (0,))
NT = ((1,), (1,))
TN = ((0,), (0,))


def params(**more):
    return pltpu.CompilerParams(vmem_limit_bytes=56 << 20, **more)


def normalize(values):
    center = values - jnp.mean(values, axis=-1, keepdims=True)
    inverse = lax.rsqrt(jnp.mean(center * center, axis=-1, keepdims=True) + EPS)
    return center * inverse, inverse


def split3(x):
    a = x.astype(BF16)
    r = x - a.astype(F32)
    b = r.astype(BF16)
    return a, b, (r - b.astype(F32)).astype(BF16)


def pack(rows):
    n = rows.shape[0] // 8
    pieces = rows.reshape(n, 8, D)
    return jnp.concatenate([pieces[:, :, : D // 2], pieces[:, :, D // 2 :]], axis=1).astype(BF16)


def unpack(pieces):
    wide = pieces.astype(F32)
    n = wide.shape[0]
    return jnp.concatenate([wide[:, :8], wide[:, 8:]], axis=2).reshape(8 * n, D)


def pair_barrier(me, core, extra=()):
    barrier = pltpu.get_barrier_semaphore()
    parity = lax.rem(core + me, 2)

    def greet(i, carry):
        other = 2 * lax.rem(lax.div(me, 2) + i, PAIRS) + parity
        pl.semaphore_signal(barrier, inc=1, device_id=(other, core), device_id_type=MESH)
        return carry

    lax.fori_loop(1, PAIRS, greet, 0)

    @pl.when(core == 1)
    def _():
        other = 2 * lax.div(me, 2) + parity
        pl.semaphore_signal(barrier, inc=1, device_id=(other, core), device_id_type=MESH)

    pl.semaphore_signal(barrier, inc=1, device_id=(me, 1 - core), device_id_type=MESH)
    for other in extra:
        pl.semaphore_signal(barrier, inc=1, device_id=(other, core), device_id_type=MESH)
    pl.semaphore_wait(barrier, PAIRS + core + len(extra))


def pair_sends(me, core, out, landing, send_sem, recv_sem):
    parity = lax.rem(core + me, 2)
    mine = lax.div(me, 2)

    def push(place):
        pltpu.make_async_remote_copy(
            src_ref=out.at[place],
            dst_ref=landing.at[core, mine],
            send_sem=send_sem,
            recv_sem=recv_sem,
            device_id=(2 * place + parity, core),
            device_id_type=MESH,
        ).start()

    @pl.when(core == 0)
    def _():
        pltpu.make_async_copy(out.at[mine], landing.at[core, mine], recv_sem).start()

    @pl.when(core == 1)
    def _():
        push(mine)

    def step(i, carry):
        push(lax.rem(mine + i, PAIRS))
        return carry

    lax.fori_loop(1, PAIRS, step, 0)


def pair_arrived(core, landing, recv_sem):
    pltpu.make_async_copy(landing.at[core], landing.at[core], recv_sem).wait()


def pair_sent(core, out, send_sem):
    most = out.at[pl.ds(0, PAIRS - 1)]
    pltpu.make_async_copy(most, most, send_sem).wait()

    @pl.when(core == 1)
    def _():
        pltpu.make_async_copy(out.at[0], out.at[0], send_sem).wait()


def to_sibling(me, core, landing, send_sem, recv_sem):
    return pltpu.make_async_remote_copy(
        src_ref=landing.at[core],
        dst_ref=landing.at[core],
        send_sem=send_sem,
        recv_sem=recv_sem,
        device_id=(me, 1 - core),
        device_id_type=MESH,
    )


def sibling_arrived(core, landing, recv_sem):
    pltpu.make_async_copy(landing.at[1 - core], landing.at[1 - core], recv_sem).wait()


def slot_rows(patch, me):
    member = (lax.broadcasted_iota(jnp.int32, (128, ROWS), 0) == patch).astype(BF16)
    before = (
        lax.broadcasted_iota(jnp.int32, (ROWS, ROWS), 0)
        < lax.broadcasted_iota(jnp.int32, (ROWS, ROWS), 1)
    ).astype(BF16)
    earlier = dot(member, before, NN)
    within = jnp.sum(earlier * member.astype(F32), axis=0, keepdims=True).astype(jnp.int32)
    return ((patch + me) & 1) * (PATCH // 2) + (patch >> 1) * 8 + within


def dispatch_kernel(
    points, cotangent, patch, rows_out, upstream_out, bias_out, slot_out,
    out_p, out_c, land_p, land_c, send_sem, recv_sem,
):
    me, core = lax.axis_index("dp"), lax.axis_index("mp")
    slot = slot_rows(patch[...], me)
    slot_out[...] = jnp.broadcast_to(slot, (8, ROWS))
    place = lax.broadcasted_iota(jnp.int32, (PATCH // 2, ROWS), 0) + core * (PATCH // 2)
    chosen = (place == slot).astype(BF16)
    filled = dot(chosen, jnp.ones((ROWS, 128), BF16), NN)
    fill = EMPTY * (1.0 - jnp.concatenate([filled] * (D // 128), axis=1))
    out_p[...] = pack(dot(chosen, points[...], NN) + fill)
    pair_barrier(me, core)
    pair_sends(me, core, out_p, land_p, send_sem.at[0], recv_sem.at[0])
    out_c[...] = pack(dot(chosen, cotangent[...], NN))
    pair_sends(me, core, out_c, land_c, send_sem.at[1], recv_sem.at[1])
    pair_arrived(core, land_p, recv_sem.at[0])
    first = to_sibling(me, core, land_p, send_sem.at[2], recv_sem.at[2])
    first.start()
    pair_arrived(core, land_c, recv_sem.at[1])
    second = to_sibling(me, core, land_c, send_sem.at[3], recv_sem.at[3])
    second.start()
    sibling_arrived(core, land_p, recv_sem.at[2])
    ones = jnp.ones((16, 128), BF16)
    for half in range(2):
        for part in range(2):
            pieces = slice(part * 32, part * 32 + 32)
            at = half * 512 + part * 256
            wide = unpack(land_p[half, pieces])
            empty = wide > 0.5 * EMPTY
            rows_out[at : at + 256, :] = jnp.where(empty, 0.0, wide).astype(BF16)
            count = dot(ones, jnp.where(empty[:, :128], 1.0, 0.0).astype(BF16), NT)
            first_row = lax.broadcasted_iota(jnp.int32, (16, 256), 0) == 0
            bias_out[:, at : at + 256] = jnp.where(
                first_row & (count > 0.5), MASKED, 0.0
            ).astype(BF16)
    sibling_arrived(core, land_c, recv_sem.at[3])
    for half in range(2):
        for part in range(2):
            pieces = slice(part * 32, part * 32 + 32)
            at = half * 512 + part * 256
            upstream_out[at : at + 256, :] = unpack(land_c[half, pieces]).astype(BF16)
    first.wait_send()
    second.wait_send()
    pair_sent(core, out_p, send_sem.at[0])
    pair_sent(core, out_c, send_sem.at[1])


def dispatch(points, cotangent, patch):
    pieces = pltpu.VMEM((PAIRS, 16, D // 2), BF16)
    landing = pltpu.VMEM((2, PAIRS, 16, D // 2), BF16)
    return pl.pallas_call(
        dispatch_kernel,
        out_shape=(
            jax.ShapeDtypeStruct((PATCH, D), BF16),
            jax.ShapeDtypeStruct((PATCH, D), BF16),
            jax.ShapeDtypeStruct((16, PATCH), BF16),
            jax.ShapeDtypeStruct((8, ROWS), jnp.int32),
        ),
        in_specs=[VMEM] * 3,
        out_specs=(VMEM,) * 4,
        scratch_shapes=[
            pieces,
            pieces,
            landing,
            landing,
            pltpu.SemaphoreType.DMA((4,)),
            pltpu.SemaphoreType.DMA((4,)),
        ],
        compiler_params=params(collective_id=1, has_side_effects=True),
        name="dispatch",
    )(points, cotangent, patch)


def forward_head(query, key, value, bias):
    scaled = split3(query.astype(F32) * EXP2_SCALE)
    wide_query = jnp.concatenate([*scaled, jnp.ones((16, PATCH), BF16)], axis=0)
    wide_key = jnp.concatenate([key, key, key, bias], axis=0)
    scores = dot(wide_key, wide_query, TN)
    maxima = jnp.max(scores, axis=0, keepdims=True)
    weights = jnp.exp2(scores - maxima)
    totals = jnp.sum(weights, axis=0, keepdims=True)
    result = dot(value, weights.astype(BF16), NN) / totals
    return result.astype(BF16), maxima + jnp.log2(totals)


def attend_kernel(rows, weight, bias, normed_out, qkv_out, attended_out, lse_out):
    for part in range(4):
        at = slice(part * 256, part * 256 + 256)
        normed, _ = normalize(rows[at, :].astype(F32))
        normed_out[at, :] = normed.astype(BF16)
    for j in range(3):
        projected = dot(weight[j * 256 : j * 256 + 256, :], normed_out[...], NT)
        qkv_out[j] = projected.astype(BF16).reshape(HEADS, HEAD_DIM, PATCH)
    mask = bias[...]

    def pair(i, carry):
        for u in range(2):
            h = 2 * i + u
            result, lse = forward_head(qkv_out[0, h], qkv_out[1, h], qkv_out[2, h], mask)
            attended_out[h] = result
            lse_out[h] = jnp.broadcast_to(lse, (8, PATCH))
        return carry

    lax.fori_loop(0, HEADS // 2, pair, 0)


def attend(rows, weight, bias):
    heads = (HEADS, HEAD_DIM, PATCH)
    return pl.pallas_call(
        attend_kernel,
        out_shape=(
            jax.ShapeDtypeStruct((PATCH, D), BF16),
            jax.ShapeDtypeStruct((3, *heads), BF16),
            jax.ShapeDtypeStruct(heads, BF16),
            jax.ShapeDtypeStruct((HEADS, 8, PATCH), F32),
        ),
        in_specs=[VMEM] * 3,
        out_specs=(VMEM,) * 4,
        compiler_params=params(),
        name="attend",
    )(rows, weight, bias)


def backward_head(query, key, value, bias, attended, upstream, lse):
    shape = (16, PATCH)
    row = lax.broadcasted_iota(jnp.int32, shape, 0)
    one = jnp.ones(shape, BF16)
    zero = jnp.zeros(shape, BF16)

    def stacked(*given):
        total = zero
        for at, value_at in enumerate(given):
            total = jnp.where(row == at, value_at, total)
        return total

    lse_pieces = split3(-jnp.broadcast_to(lse, shape))
    scaled = split3(query.astype(F32) * EXP2_SCALE)
    wide_query = jnp.concatenate([*scaled, stacked(one, *lse_pieces)], axis=0)
    wide_key = jnp.concatenate([key, key, key, stacked(bias, one, one, one)], axis=0)
    scale = HEAD_DIM**-0.5
    upstream_wide = upstream.astype(F32)
    delta = -scale * jnp.sum(upstream_wide * attended.astype(F32), axis=0, keepdims=True)
    delta_pieces = split3(jnp.broadcast_to(delta, shape))
    wide_upstream = jnp.concatenate(
        [(scale * upstream_wide).astype(BF16), stacked(*delta_pieces)], axis=0
    )
    wide_value = jnp.concatenate([value, stacked(one, one, one)], axis=0)
    d_query, d_key, d_value = [], None, None
    for part in range(2):
        at = slice(part * 512, part * 512 + 512)
        weights = jnp.exp2(dot(wide_query[:, at], wide_key, TN))
        d_scores = (weights * dot(wide_upstream[:, at], wide_value, TN)).astype(BF16)
        d_query.append(dot(key, d_scores, NT))
        more_key = dot(query[:, at], d_scores, NN)
        more_value = dot(upstream[:, at], weights.astype(BF16), NN)
        d_key = more_key if d_key is None else d_key + more_key
        d_value = more_value if d_value is None else d_value + more_value
    return jnp.concatenate(d_query, axis=1).astype(BF16), d_key.astype(BF16), d_value.astype(BF16)


def gelu_both(values):
    squared = values * values
    tangent = jnp.tanh(GELU_C * (values + 0.044715 * squared * values))
    half = 0.5 * (1.0 + tangent)
    derivative = half + 0.5 * values * (1.0 - tangent * tangent) * GELU_C * (
        1.0 + 3.0 * 0.044715 * squared
    )
    return values * half, derivative


CHUNK = 256


def row_order():
    place = lax.broadcasted_iota(jnp.int32, (D, D), 1)
    y, z, x, j = place >> 7, (place >> 4) & 7, (place >> 2) & 3, place & 3
    channel = (z << 6) + (x << 4) + (y << 2) + j
    return (lax.broadcasted_iota(jnp.int32, (D, D), 0) == channel).astype(BF16)


def feed_forward_kernel(
    attended, rows, upstream, proj, fc1, fc2, block_out, grad_a, grad_b, d_attended_out,
    snd1, rcv1, snd2, rcv2, snd3, rcv3, own2, mixed, normed_mid, inverse, act, d_pre, d_mixed,
    permuted,
    send_sem, recv_sem,
):
    me, core = lax.axis_index("dp"), lax.axis_index("mp")
    sibling = (me, 1 - core)
    barrier = pltpu.get_barrier_semaphore()
    pl.semaphore_signal(barrier, inc=1, device_id=sibling, device_id_type=MESH)
    chunks = PATCH // CHUNK

    def place(i):
        return lax.rem(i + 2 * (1 - core), chunks)

    def span(k):
        return pl.ds(pl.multiple_of(k * CHUNK, CHUNK), CHUNK)

    def copy(kind, i, src, dst):
        return pltpu.make_async_remote_copy(
            src_ref=src,
            dst_ref=dst,
            send_sem=send_sem.at[kind, i],
            recv_sem=recv_sem.at[kind, i],
            device_id=sibling,
            device_id_type=MESH,
        )

    def copy1(k):
        return copy(0, k, snd1.at[span(k), :], rcv1.at[span(k), :])

    def copy2(i):
        at = pl.ds(i * CHUNK, CHUNK)
        return copy(1, i, snd2.at[at, :], rcv2.at[at, :])

    def copy3(k):
        return copy(2, k, snd3.at[span(k), :], rcv3.at[span(k), :])

    for k in range(chunks):
        partial = dot(attended[:, k * CHUNK : (k + 1) * CHUNK], proj[...], TN)
        snd1[k * CHUNK : (k + 1) * CHUNK, :] = partial.astype(BF16)
        if k == 0:
            pl.semaphore_wait(barrier, 1)
        copy1(k).start()

    for i in range(chunks):
        k = place(i)
        at = span(k)
        copy1(k).wait_recv()
        total = rows[at, :].astype(F32) + (snd1[at, :].astype(F32) + rcv1[at, :].astype(F32))
        mixed[at, :] = total
        normed, inv = normalize(total)
        inverse[at, :] = jnp.broadcast_to(inv, (CHUNK, 128))
        low = normed.astype(BF16)
        normed_mid[at, :] = low
        activation, derivative = gelu_both(dot(low, fc1[...], NN))
        act_low = activation.astype(BF16)
        act[at, :] = act_low
        partial = dot(act_low, fc2[...], NN).astype(BF16)
        if i < 2:
            snd2[i * CHUNK : (i + 1) * CHUNK, :] = partial
            copy2(i).start()
        else:
            own2[(i - 2) * CHUNK : (i - 1) * CHUNK, :] = partial
        d_low = (dot(upstream[at, :], fc2[...], NT) * derivative).astype(BF16)
        d_pre[at, :] = d_low
        snd3[at, :] = dot(d_low, fc1[...], NT).astype(BF16)
        copy3(k).start()

    permuted[...] = dot(upstream[...], row_order(), NN).astype(BF16)
    for part in range(4):
        cols = slice(part * 256, part * 256 + 256)
        grad_a[:, cols] = dot(normed_mid[...], d_pre[:, cols], TN).astype(BF16)
        grad_b[:, cols] = dot(permuted[...], act[:, cols], TN).astype(BF16)

    for i in range(chunks):
        k = place(i)
        at = span(k)
        copy3(k).wait_recv()
        back = snd3[at, :].astype(F32) + rcv3[at, :].astype(F32)
        inv = inverse[at, :][:, 0:1]
        total = mixed[at, :]
        center = total - jnp.mean(total, axis=-1, keepdims=True)
        normed = center * inv
        mean_grad = jnp.mean(back, axis=-1, keepdims=True)
        mean_mixed = jnp.mean(back * normed, axis=-1, keepdims=True)
        through = inv * (back - mean_grad - normed * mean_mixed)
        d_mixed[at, :] = (upstream[at, :].astype(F32) + through).astype(BF16)

    for k in range(chunks):
        at = slice(k * CHUNK, (k + 1) * CHUNK)
        d_attended_out[:, at] = dot(proj[...], d_mixed[at, :], NT).astype(BF16)
    grad_a[:, 1024:1280] = dot(attended[...], d_mixed[...], NN).T.astype(BF16)

    for i in range(2):
        copy2(i).wait_recv()
        own = slice(i * CHUNK, (i + 1) * CHUNK)
        total = mixed[span(place(i + 2)), :] + (own2[own, :].astype(F32) + rcv2[own, :].astype(F32))
        block_out[i * 32 : i * 32 + 32] = pack(total.astype(BF16).astype(F32))
    for k in range(chunks):
        copy1(k).wait_send()
        copy3(k).wait_send()
    for i in range(2):
        copy2(i).wait_send()


def feed_forward(attended, rows, upstream, proj, fc1, fc2):
    whole = pltpu.VMEM((PATCH, D), BF16)
    half = pltpu.VMEM((PATCH // 2, D), BF16)
    return pl.pallas_call(
        feed_forward_kernel,
        out_shape=(
            jax.ShapeDtypeStruct((PAIRS, 16, D // 2), BF16),
            jax.ShapeDtypeStruct((D, AW), BF16),
            jax.ShapeDtypeStruct((D, BW), BF16),
            jax.ShapeDtypeStruct((256, PATCH), BF16),
        ),
        in_specs=[VMEM] * 6,
        out_specs=(VMEM,) * 4,
        scratch_shapes=[
            whole,
            whole,
            half,
            half,
            whole,
            whole,
            half,
            pltpu.VMEM((PATCH, D), F32),
            whole,
            pltpu.VMEM((PATCH, 128), F32),
            pltpu.VMEM((PATCH, FF), BF16),
            pltpu.VMEM((PATCH, FF), BF16),
            whole,
            whole,
            pltpu.SemaphoreType.DMA((3, 4)),
            pltpu.SemaphoreType.DMA((3, 4)),
        ],
        compiler_params=params(collective_id=2, has_side_effects=True),
        name="feed_forward",
    )(attended, rows, upstream, proj, fc1, fc2)


class ReduceScatter:
    def __init__(self, me, core, x_first, grad, scratch):
        z, x, y = lax.div(me, NX * NY), lax.rem(lax.div(me, NY), NX), lax.rem(me, NY)
        at_x = [(z * NX + lax.rem(x + d, NX)) * NY + y for d in range(NX)]
        at_z = [(lax.rem(z + d, NZ) * NX + x) * NY + y for d in range(NZ)]
        at_y = [(z * NX + x) * NY + lax.rem(y + d, NY) for d in range(NY)]
        self.core, self.x_first = core, x_first
        self.peers = (at_x, at_z, at_y) if x_first else (at_y, at_z, at_x)
        self.place = (x, z, y) if x_first else (y, z, x)
        self.grad = grad
        self.land_0, self.mid, self.land_1, self.low, self.land_2, self.send, self.recv = scratch

    def copy(self, phase, d, src, dst):
        base = (0, NX - 1, NX + NZ - 2)[phase]
        return pltpu.make_async_remote_copy(
            src_ref=src,
            dst_ref=dst,
            send_sem=self.send.at[base + d - 1],
            recv_sem=self.recv.at[base + d - 1],
            device_id=(self.peers[phase][d], self.core),
            device_id_type=MESH,
        )

    def piece(self, d):
        at = lax.rem(self.place[0] + d, NX)
        return self.grad.at[:, at] if self.x_first else self.grad.at[at]

    def copies(self, phase):
        if phase == 0:
            return [self.copy(0, d, self.piece(d), self.land_0.at[d - 1]) for d in range(1, NX)]
        if phase == 1:
            z = self.place[1]
            return [
                self.copy(1, d, self.mid.at[lax.rem(z + d, NZ)], self.land_1.at[d - 1])
                for d in range(1, NZ)
            ]
        return [self.copy(2, d, self.low, self.land_2.at[d - 1]) for d in range(1, NY)]

    def start(self, phase=0):
        for one in self.copies(phase):
            one.start()

    def arrived(self, phase):
        for one in self.copies(phase):
            one.wait_recv()

    def second(self):
        self.arrived(0)
        mine = self.place[0]

        def step(i, carry):
            own = self.grad[i, mine] if self.x_first else self.grad[mine, i]
            total = own.astype(F32)
            for d in range(NX - 1):
                total = total + self.land_0[d, i].astype(F32)
            self.mid[i] = total.astype(BF16)
            return carry

        lax.fori_loop(0, NZ, step, 0)
        self.start(1)

    def third(self):
        self.arrived(1)
        total = self.mid[self.place[1]].astype(F32)
        for d in range(NZ - 1):
            total = total + self.land_1[d].astype(F32)
        self.low[...] = total.astype(BF16)
        self.start(2)

    def result(self):
        self.arrived(2)
        total = self.low[...].astype(F32)
        for d in range(NY - 1):
            total = total + self.land_2[d].astype(F32)
        result = total[0:4]
        for other in range(1, NY):
            part = total[4 * other : 4 * other + 4]
            result = jnp.where(self.place[2] == other, part, result)
        return result

    def finish(self):
        for phase in range(3):
            for one in self.copies(phase):
                one.wait_send()


def reduce_scratch(columns):
    return [
        pltpu.VMEM((NX - 1, NZ, 16, columns), BF16),
        pltpu.VMEM((NZ, 16, columns), BF16),
        pltpu.VMEM((NZ - 1, 16, columns), BF16),
        pltpu.VMEM((16, columns), BF16),
        pltpu.VMEM((NY - 1, 16, columns), BF16),
        pltpu.SemaphoreType.DMA((NX + NY + NZ - 3,)),
        pltpu.SemaphoreType.DMA((NX + NY + NZ - 3,)),
    ]


def attend_back_kernel(
    block, grad_a, grad_b, normed, qkv, bias, attended, upstream, lse,
    land, sums_a, sums_b, sums_qa, sums_qb,
    d_qkv, grad_qa, grad_qb, send_sem, recv_sem, *scratch,
):
    me, core = lax.axis_index("dp"), lax.axis_index("mp")
    parts = [
        ReduceScatter(me, core, first, grad, scratch[7 * i : 7 * i + 7])
        for i, (first, grad) in enumerate(
            ((True, grad_a), (False, grad_b), (True, grad_qa), (True, grad_qb))
        )
    ]
    part_a, part_b, part_qa, part_qb = parts
    swap = to_sibling(me, core, land, send_sem.at[1], recv_sem.at[1])
    pair_barrier(me, core, [p for axis in part_a.peers for p in axis[1:]])
    part_a.start()
    part_b.start()
    pair_sends(me, core, block, land, send_sem.at[0], recv_sem.at[0])
    mask = bias[...]

    def project(first, last, out):
        rows = (last - first) * HEAD_DIM
        heads = [d_qkv[j, first:last].reshape(rows, PATCH) for j in range(3)]
        grad = dot(jnp.concatenate(heads, axis=0), normed[...], NN)
        out[...] = grad.T.astype(BF16).reshape(out.shape)

    def one_head(h, carry):
        @pl.when(h == 6)
        def _():
            part_a.second()
            part_b.second()

        @pl.when(h == 11)
        def _():
            part_a.third()
            part_b.third()

        @pl.when(h == FIRST_HEADS)
        def _():
            project(0, FIRST_HEADS, grad_qa)
            part_qa.start()
            pair_arrived(core, land, recv_sem.at[0])
            swap.start()

        @pl.when(h == 15)
        def _():
            part_qa.second()

        d_query, d_key, d_value = backward_head(
            qkv[0, h], qkv[1, h], qkv[2, h], mask, attended[h], upstream[h], lse[h][0:1]
        )
        d_qkv[0, h] = d_query
        d_qkv[1, h] = d_key
        d_qkv[2, h] = d_value
        return carry

    lax.fori_loop(0, HEADS, one_head, 0)
    project(FIRST_HEADS, HEADS, grad_qb)
    part_qb.start()
    part_qa.third()
    sums_a[...] = part_a.result()
    sums_b[...] = part_b.result()
    part_qb.second()
    sibling_arrived(core, land, recv_sem.at[1])
    part_qb.third()
    sums_qa[...] = part_qa.result()
    swap.wait_send()
    pair_sent(core, block, send_sem.at[0])
    sums_qb[...] = part_qb.result()
    for part in parts:
        part.finish()


def attend_back(block, grad_a, grad_b, normed, qkv, bias, attended, upstream, lse):
    return pl.pallas_call(
        attend_back_kernel,
        out_shape=(
            jax.ShapeDtypeStruct((2, PAIRS, 16, D // 2), BF16),
            jax.ShapeDtypeStruct((4, AW), F32),
            jax.ShapeDtypeStruct((4, BW), F32),
            jax.ShapeDtypeStruct((4, QA), F32),
            jax.ShapeDtypeStruct((4, QB), F32),
        ),
        in_specs=[VMEM] * 9,
        out_specs=(VMEM,) * 5,
        scratch_shapes=[
            pltpu.VMEM((3, HEADS, HEAD_DIM, PATCH), BF16),
            pltpu.VMEM((NZ, NX, 16, QA), BF16),
            pltpu.VMEM((NZ, NX, 16, QB), BF16),
            pltpu.SemaphoreType.DMA((2,)),
            pltpu.SemaphoreType.DMA((2,)),
            *reduce_scratch(AW),
            *reduce_scratch(BW),
            *reduce_scratch(QA),
            *reduce_scratch(QB),
        ],
        compiler_params=params(collective_id=3, has_side_effects=True),
        name="attend_back",
    )(
        block,
        grad_a.reshape(NZ, NX, 16, AW),
        grad_b.reshape(NY, NZ, 16, BW),
        normed,
        qkv,
        bias,
        attended,
        upstream,
        lse,
    )


def finish_kernel(
    land, slot, sums_a, sums_b, sums_qa, sums_qb, rows_out, qkv_out, proj_out, fc1_out, fc2_out
):
    total = None
    for half in range(2):
        place = lax.broadcasted_iota(jnp.int32, (PATCH // 2, ROWS), 0) + half * (PATCH // 2)
        chosen = (place == slot[0:1, :]).astype(BF16)
        part = dot(chosen, unpack(land[half]).astype(BF16), TN)
        total = part if total is None else total + part
    rows_out[...] = total.astype(BF16)

    def turned(rows):
        return jnp.concatenate([rows, rows], axis=0).T[:, 0:4]

    fc1_out[...] = sums_a[:, :FF]
    proj_out[...] = turned(sums_a[:, FF:])
    fc2_out[...] = turned(sums_b[...])
    first, last = sums_qa[...], sums_qb[...]
    n, m = QA // 3, QB // 3
    for j in range(3):
        both = jnp.concatenate(
            [first[:, j * n : (j + 1) * n], last[:, j * m : (j + 1) * m]], axis=1
        )
        for i in range(4):
            qkv_out[i, j : j + 1, :] = both[i : i + 1, :]


def finish(*given):
    return pl.pallas_call(
        finish_kernel,
        out_shape=(
            jax.ShapeDtypeStruct((ROWS, D), BF16),
            jax.ShapeDtypeStruct((4, 3, 256), F32),
            jax.ShapeDtypeStruct((256, 4), F32),
            jax.ShapeDtypeStruct((4, FF), F32),
            jax.ShapeDtypeStruct((FF, 4), F32),
        ),
        in_specs=[VMEM] * 6,
        out_specs=(VMEM,) * 5,
        compiler_params=params(),
        name="finish",
    )(*given)


def per_device(points, patch_of, qkv_weight, proj_weight, fc1_weight, fc2_weight, cotangent):
    weight = qkv_weight.reshape(D, 3 * 256).T
    rows, upstream, bias, slot = dispatch(points, cotangent, patch_of.reshape(1, ROWS))
    normed, qkv, attended, lse = attend(rows, weight, bias)
    block, grad_a, grad_b, d_attended = feed_forward(
        attended.reshape(256, PATCH), rows, upstream, proj_weight, fc1_weight, fc2_weight
    )
    d_attended = d_attended.reshape(HEADS, HEAD_DIM, PATCH)
    land, *sums = attend_back(
        block, grad_a, grad_b, normed, qkv, bias, attended, d_attended, lse
    )
    return tuple(finish(land, slot, *sums))


def solution(mesh):
    placed = (
        P("dp", None),
        P("dp", None),
        P(None, None, "mp"),
        P("mp", None),
        P(None, "mp"),
        P("mp", None),
        P("dp", None),
    )
    return jax.shard_map(
        per_device,
        mesh=mesh,
        in_specs=placed,
        out_specs=(P("dp", None), P("dp", None, "mp"), P("mp", "dp"), P("dp", "mp"), P("mp", "dp")),
        check_vma=False,
    )
```

```python
import math
import types

import jax
import jax.numpy as jnp
from jax import lax
from jax.experimental import pallas as pl
from jax.experimental.pallas import tpu as pltpu
from jax.sharding import PartitionSpec as P

MESH = pl.DeviceIdType.MESH
F32 = jnp.float32
BF16 = jnp.bfloat16
VMEM = pl.BlockSpec(memory_space=pltpu.VMEM)

HEADS = 16
HEAD_DIM = 16
PATCH = 1024
ROWS = 512
D = 512
FF = 1024
EPS = 1e-05
GELU_C = math.sqrt(2.0 / math.pi)
EXP2_SCALE = HEAD_DIM**-0.5 * math.log2(math.e)
EMPTY = 64.0
MASKED = -1e30
NX, NY, NZ = 4, 4, 8
PAIRS = 64
FIRST_HEADS = 12
AW = 1280
BW = 1024
QA = 3 * HEAD_DIM * FIRST_HEADS
QB = 3 * HEAD_DIM * (HEADS - FIRST_HEADS)


def dot(left, right, dims):
    return lax.dot_general(left, right, (dims, ((), ())), preferred_element_type=F32)


NN = ((1,), (0,))
NT = ((1,), (1,))
TN = ((0,), (0,))


def params(**more):
    return pltpu.CompilerParams(vmem_limit_bytes=60 << 20, **more)


def normalize(values):
    center = values - jnp.mean(values, axis=-1, keepdims=True)
    inverse = lax.rsqrt(jnp.mean(center * center, axis=-1, keepdims=True) + EPS)
    return center * inverse, inverse


def split3(x):
    a = x.astype(BF16)
    r = x - a.astype(F32)
    b = r.astype(BF16)
    return a, b, (r - b.astype(F32)).astype(BF16)


def pack(rows):
    n = rows.shape[0] // 8
    pieces = rows.reshape(n, 8, D)
    return jnp.concatenate([pieces[:, :, : D // 2], pieces[:, :, D // 2 :]], axis=1).astype(BF16)


def unpack(pieces):
    wide = pieces.astype(F32)
    n = wide.shape[0]
    return jnp.concatenate([wide[:, :8], wide[:, 8:]], axis=2).reshape(8 * n, D)


def pair_greet(me, core, extra=()):
    barrier = pltpu.get_barrier_semaphore()
    parity = lax.rem(core + me, 2)

    def greet(i, carry):
        other = 2 * lax.rem(lax.div(me, 2) + i, PAIRS) + parity
        pl.semaphore_signal(barrier, inc=1, device_id=(other, core), device_id_type=MESH)
        return carry

    lax.fori_loop(1, PAIRS, greet, 0)

    @pl.when(core == 1)
    def _():
        other = 2 * lax.div(me, 2) + parity
        pl.semaphore_signal(barrier, inc=1, device_id=(other, core), device_id_type=MESH)

    pl.semaphore_signal(barrier, inc=1, device_id=(me, 1 - core), device_id_type=MESH)
    for other in extra:
        pl.semaphore_signal(barrier, inc=1, device_id=(other, core), device_id_type=MESH)


def pair_greeted(core, extra=()):
    pl.semaphore_wait(pltpu.get_barrier_semaphore(), PAIRS + core + len(extra))


def pair_sends(me, core, out, landing, send_sem, recv_sem):
    parity = lax.rem(core + me, 2)
    mine = lax.div(me, 2)

    def push(place):
        pltpu.make_async_remote_copy(
            src_ref=out.at[place],
            dst_ref=landing.at[core, mine],
            send_sem=send_sem,
            recv_sem=recv_sem,
            device_id=(2 * place + parity, core),
            device_id_type=MESH,
        ).start()

    @pl.when(core == 0)
    def _():
        pltpu.make_async_copy(out.at[mine], landing.at[core, mine], recv_sem).start()

    @pl.when(core == 1)
    def _():
        push(mine)

    def step(i, carry):
        push(lax.rem(mine + i, PAIRS))
        return carry

    lax.fori_loop(1, PAIRS, step, 0)


def pair_arrived(core, landing, recv_sem):
    pltpu.make_async_copy(landing.at[core], landing.at[core], recv_sem).wait()


def pair_sent(core, out, send_sem):
    most = out.at[pl.ds(0, PAIRS - 1)]
    pltpu.make_async_copy(most, most, send_sem).wait()

    @pl.when(core == 1)
    def _():
        pltpu.make_async_copy(out.at[0], out.at[0], send_sem).wait()


def to_sibling(me, core, landing, send_sem, recv_sem):
    return pltpu.make_async_remote_copy(
        src_ref=landing.at[core],
        dst_ref=landing.at[core],
        send_sem=send_sem,
        recv_sem=recv_sem,
        device_id=(me, 1 - core),
        device_id_type=MESH,
    )


def sibling_arrived(core, landing, recv_sem):
    pltpu.make_async_copy(landing.at[1 - core], landing.at[1 - core], recv_sem).wait()


def slot_rows(patch, me):
    member = (lax.broadcasted_iota(jnp.int32, (128, ROWS), 0) == patch).astype(BF16)
    before = (
        lax.broadcasted_iota(jnp.int32, (ROWS, ROWS), 0)
        < lax.broadcasted_iota(jnp.int32, (ROWS, ROWS), 1)
    ).astype(BF16)
    earlier = dot(member, before, NN)
    within = jnp.sum(earlier * member.astype(F32), axis=0, keepdims=True).astype(jnp.int32)
    return ((patch + me) & 1) * (PATCH // 2) + (patch >> 1) * 8 + within


def forward_head(query, key, value, bias):
    scaled = split3(query.astype(F32) * EXP2_SCALE)
    wide_query = jnp.concatenate([*scaled, jnp.ones((16, PATCH), BF16)], axis=0)
    wide_key = jnp.concatenate([key, key, key, bias], axis=0)
    scores = dot(wide_key, wide_query, TN)
    maxima = jnp.max(scores, axis=0, keepdims=True)
    weights = jnp.exp2(scores - maxima)
    totals = jnp.sum(weights, axis=0, keepdims=True)
    result = dot(value, weights.astype(BF16), NN) / totals
    return result.astype(BF16), maxima + jnp.log2(totals)


def dispatch_and_attend(me, core, ref, others):
    pair_greet(me, core, others)
    slot = slot_rows(ref.patch[...], me)
    ref.slot_out[...] = jnp.broadcast_to(slot, (8, ROWS))
    place = lax.broadcasted_iota(jnp.int32, (PATCH // 2, ROWS), 0) + core * (PATCH // 2)
    chosen = (place == slot).astype(BF16)
    filled = dot(chosen, jnp.ones((ROWS, 128), BF16), NN)
    fill = EMPTY * (1.0 - jnp.concatenate([filled] * (D // 128), axis=1))
    ref.out_p[...] = pack(dot(chosen, ref.points[...], NN) + fill)
    pair_greeted(core, others)
    send, recv = ref.pair_send, ref.pair_recv
    pair_sends(me, core, ref.out_p, ref.land_p, send.at[0], recv.at[0])
    ref.out_c[...] = pack(dot(chosen, ref.cotangent[...], NN))
    swap_p = to_sibling(me, core, ref.land_p, send.at[2], recv.at[2])
    swap_c = to_sibling(me, core, ref.land_c, send.at[3], recv.at[3])
    pair_arrived(core, ref.land_p, recv.at[0])
    swap_p.start()
    pair_sends(me, core, ref.out_c, ref.land_c, send.at[1], recv.at[1])
    ones = jnp.ones((16, 128), BF16)

    def receive(half):
        for part in range(2):
            start = pl.multiple_of(half * 512 + part * 256, 256)
            at = pl.ds(start, 256)
            wide = unpack(ref.land_p[half, part * 32 : part * 32 + 32])
            empty = wide > 0.5 * EMPTY
            real = jnp.where(empty, 0.0, wide)
            ref.rows[at, :] = real.astype(BF16)
            count = dot(ones, jnp.where(empty[:, :128], 1.0, 0.0).astype(BF16), NT)
            first_row = lax.broadcasted_iota(jnp.int32, (16, 256), 0) == 0
            ref.bias[:, at] = jnp.where(first_row & (count > 0.5), MASKED, 0.0).astype(BF16)
            normed = normalize(real)[0].astype(BF16)
            ref.normed[at, :] = normed
            for j in range(3):
                projected = dot(ref.weight[j], normed, ((0,), (1,))).astype(BF16)
                ref.qkv[j, :, :, at] = projected.reshape(HEADS, HEAD_DIM, 256)

    receive(core)
    sibling_arrived(core, ref.land_p, recv.at[2])
    receive(1 - core)
    mask = ref.bias[...]

    def pair(i, carry):
        @pl.when(i == 6)
        def _():
            pair_arrived(core, ref.land_c, recv.at[1])
            swap_c.start()

        for u in range(2):
            h = 2 * i + u
            result, lse = forward_head(ref.qkv[0, h], ref.qkv[1, h], ref.qkv[2, h], mask)
            ref.attended[h] = result
            ref.lse[h] = jnp.broadcast_to(lse, (8, PATCH))
        return carry

    lax.fori_loop(0, HEADS // 2, pair, 0)

    def upstream_arrived():
        sibling_arrived(core, ref.land_c, recv.at[3])
        for half in range(2):
            for part in range(2):
                at = half * 512 + part * 256
                pieces = ref.land_c[half, part * 32 : part * 32 + 32]
                ref.upstream[at : at + 256, :] = unpack(pieces).astype(BF16)

    def finish():
        swap_p.wait_send()
        swap_c.wait_send()
        pair_sent(core, ref.out_p, send.at[0])
        pair_sent(core, ref.out_c, send.at[1])

    return upstream_arrived, finish


def backward_head(query, key, value, bias, attended, upstream, lse):
    shape = (16, PATCH)
    row = lax.broadcasted_iota(jnp.int32, shape, 0)
    one = jnp.ones(shape, BF16)
    zero = jnp.zeros(shape, BF16)

    def stacked(*given):
        total = zero
        for at, value_at in enumerate(given):
            total = jnp.where(row == at, value_at, total)
        return total

    lse_pieces = split3(-jnp.broadcast_to(lse, shape))
    scaled = split3(query.astype(F32) * EXP2_SCALE)
    wide_query = jnp.concatenate([*scaled, stacked(one, *lse_pieces)], axis=0)
    wide_key = jnp.concatenate([key, key, key, stacked(bias, one, one, one)], axis=0)
    scale = HEAD_DIM**-0.5
    upstream_wide = upstream.astype(F32)
    delta = -scale * jnp.sum(upstream_wide * attended.astype(F32), axis=0, keepdims=True)
    delta_pieces = split3(jnp.broadcast_to(delta, shape))
    wide_upstream = jnp.concatenate(
        [(scale * upstream_wide).astype(BF16), stacked(*delta_pieces)], axis=0
    )
    wide_value = jnp.concatenate([value, stacked(one, one, one)], axis=0)
    d_query, d_key, d_value = [], None, None
    for part in range(2):
        at = slice(part * 512, part * 512 + 512)
        weights = jnp.exp2(dot(wide_query[:, at], wide_key, TN))
        d_scores = (weights * dot(wide_upstream[:, at], wide_value, TN)).astype(BF16)
        d_query.append(dot(key, d_scores, NT))
        more_key = dot(query[:, at], d_scores, NN)
        more_value = dot(upstream[:, at], weights.astype(BF16), NN)
        d_key = more_key if d_key is None else d_key + more_key
        d_value = more_value if d_value is None else d_value + more_value
    return jnp.concatenate(d_query, axis=1).astype(BF16), d_key.astype(BF16), d_value.astype(BF16)


def gelu_both(values):
    squared = values * values
    tangent = jnp.tanh(GELU_C * (values + 0.044715 * squared * values))
    half = 0.5 * (1.0 + tangent)
    derivative = half + 0.5 * values * (1.0 - tangent * tangent) * GELU_C * (
        1.0 + 3.0 * 0.044715 * squared
    )
    return values * half, derivative


CHUNK = 256


def row_order():
    place = lax.broadcasted_iota(jnp.int32, (D, D), 1)
    y, z, x, j = place >> 7, (place >> 4) & 7, (place >> 2) & 3, place & 3
    channel = (z << 6) + (x << 4) + (y << 2) + j
    return (lax.broadcasted_iota(jnp.int32, (D, D), 0) == channel).astype(BF16)


def feed_forward(me, core, ref, upstream_arrived, part_a, part_b):
    sibling = (me, 1 - core)
    chunks = PATCH // CHUNK
    proj, fc1, fc2 = ref.proj, ref.fc1, ref.fc2

    def place(i):
        return lax.rem(i + 2 * (1 - core), chunks)

    def span(k):
        return pl.ds(pl.multiple_of(k * CHUNK, CHUNK), CHUNK)

    def copy(kind, i, src, dst):
        return pltpu.make_async_remote_copy(
            src_ref=src,
            dst_ref=dst,
            send_sem=ref.core_send.at[kind, i],
            recv_sem=ref.core_recv.at[kind, i],
            device_id=sibling,
            device_id_type=MESH,
        )

    def copy1(k):
        return copy(0, k, ref.snd1.at[span(k), :], ref.rcv1.at[span(k), :])

    def copy2(i):
        at = pl.ds(i * CHUNK, CHUNK)
        return copy(1, i, ref.snd2.at[at, :], ref.rcv2.at[at, :])

    def copy3(k):
        return copy(2, k, ref.snd3.at[span(k), :], ref.rcv3.at[span(k), :])

    for i in range(chunks):
        k = place(i)
        heads = ref.attended[:, :, span(k)].reshape(256, CHUNK)
        ref.snd1[span(k), :] = dot(heads, proj[...], TN).astype(BF16)
        copy1(k).start()
    upstream_arrived()

    for i in range(chunks):
        k = place(i)
        at = span(k)
        copy1(k).wait_recv()
        added = ref.snd1[at, :].astype(F32) + ref.rcv1[at, :].astype(F32)
        total = ref.rows[at, :].astype(F32) + added
        ref.mixed[at, :] = total
        normed, inv = normalize(total)
        ref.inverse[at, :] = jnp.broadcast_to(inv, (CHUNK, 128))
        low = normed.astype(BF16)
        ref.normed_mid[at, :] = low
        activation, derivative = gelu_both(dot(low, fc1[...], NN))
        act_low = activation.astype(BF16)
        ref.act[at, :] = act_low
        partial = dot(act_low, fc2[...], NN).astype(BF16)
        if i < 2:
            ref.snd2[i * CHUNK : (i + 1) * CHUNK, :] = partial
            copy2(i).start()
        else:
            ref.own2[(i - 2) * CHUNK : (i - 1) * CHUNK, :] = partial
        d_low = (dot(ref.upstream[at, :], fc2[...], NT) * derivative).astype(BF16)
        ref.d_pre[at, :] = d_low
        ref.snd3[at, :] = dot(d_low, fc1[...], NT).astype(BF16)
        copy3(k).start()

    ref.permuted[...] = dot(ref.upstream[...], row_order(), NN).astype(BF16)
    for part in range(4):
        cols = slice(part * 256, part * 256 + 256)
        grad = dot(ref.permuted[...], ref.act[:, cols], TN).astype(BF16)
        ref.grad_b[:, :, :, cols] = grad.reshape(NY, NZ, 16, 256)
    part_b.start()
    for part in range(4):
        cols = slice(part * 256, part * 256 + 256)
        grad = dot(ref.normed_mid[...], ref.d_pre[:, cols], TN).astype(BF16)
        ref.grad_a[:, :, :, cols] = grad.reshape(NZ, NX, 16, 256)

    for i in range(chunks):
        k = place(i)
        at = span(k)
        copy3(k).wait_recv()
        back = ref.snd3[at, :].astype(F32) + ref.rcv3[at, :].astype(F32)
        inv = ref.inverse[at, :][:, 0:1]
        total = ref.mixed[at, :]
        center = total - jnp.mean(total, axis=-1, keepdims=True)
        normed = center * inv
        mean_grad = jnp.mean(back, axis=-1, keepdims=True)
        mean_mixed = jnp.mean(back * normed, axis=-1, keepdims=True)
        through = inv * (back - mean_grad - normed * mean_mixed)
        low = (ref.upstream[at, :].astype(F32) + through).astype(BF16)
        ref.d_mixed[at, :] = low
        heads = dot(proj[...], low, NT).astype(BF16)
        ref.d_attended[:, :, at] = heads.reshape(HEADS, HEAD_DIM, CHUNK)

    grad = dot(ref.attended[...].reshape(256, PATCH), ref.d_mixed[...], NN).T.astype(BF16)
    ref.grad_a[:, :, :, FF:AW] = grad.reshape(NZ, NX, 16, AW - FF)
    part_a.start()

    for i in range(2):
        copy2(i).wait_recv()
        own = slice(i * CHUNK, (i + 1) * CHUNK)
        added = ref.own2[own, :].astype(F32) + ref.rcv2[own, :].astype(F32)
        total = ref.mixed[span(place(i + 2)), :] + added
        ref.block[i * 32 : i * 32 + 32] = pack(total.astype(BF16).astype(F32))

    def finish():
        for k in range(chunks):
            copy1(k).wait_send()
            copy3(k).wait_send()
        for i in range(2):
            copy2(i).wait_send()

    return finish


class ReduceScatter:
    def __init__(self, me, core, x_first, grad, scratch):
        z, x, y = lax.div(me, NX * NY), lax.rem(lax.div(me, NY), NX), lax.rem(me, NY)
        at_x = [(z * NX + lax.rem(x + d, NX)) * NY + y for d in range(NX)]
        at_z = [(lax.rem(z + d, NZ) * NX + x) * NY + y for d in range(NZ)]
        at_y = [(z * NX + x) * NY + lax.rem(y + d, NY) for d in range(NY)]
        self.core, self.x_first = core, x_first
        self.peers = (at_x, at_z, at_y) if x_first else (at_y, at_z, at_x)
        self.place = (x, z, y) if x_first else (y, z, x)
        self.grad = grad
        self.land_0, self.mid, self.land_1, self.low, self.land_2, self.send, self.recv = scratch

    def copy(self, phase, d, src, dst):
        base = (0, NX - 1, NX + NZ - 2)[phase]
        return pltpu.make_async_remote_copy(
            src_ref=src,
            dst_ref=dst,
            send_sem=self.send.at[base + d - 1],
            recv_sem=self.recv.at[base + d - 1],
            device_id=(self.peers[phase][d], self.core),
            device_id_type=MESH,
        )

    def piece(self, d):
        at = lax.rem(self.place[0] + d, NX)
        return self.grad.at[:, at] if self.x_first else self.grad.at[at]

    def copies(self, phase):
        if phase == 0:
            return [self.copy(0, d, self.piece(d), self.land_0.at[d - 1]) for d in range(1, NX)]
        if phase == 1:
            z = self.place[1]
            return [
                self.copy(1, d, self.mid.at[lax.rem(z + d, NZ)], self.land_1.at[d - 1])
                for d in range(1, NZ)
            ]
        return [self.copy(2, d, self.low, self.land_2.at[d - 1]) for d in range(1, NY)]

    def start(self, phase=0):
        for one in self.copies(phase):
            one.start()

    def arrived(self, phase):
        for one in self.copies(phase):
            one.wait_recv()

    def second(self):
        self.arrived(0)
        mine = self.place[0]

        def step(i, carry):
            own = self.grad[i, mine] if self.x_first else self.grad[mine, i]
            total = own.astype(F32)
            for d in range(NX - 1):
                total = total + self.land_0[d, i].astype(F32)
            self.mid[i] = total.astype(BF16)
            return carry

        lax.fori_loop(0, NZ, step, 0)
        self.start(1)

    def third(self):
        self.arrived(1)
        total = self.mid[self.place[1]].astype(F32)
        for d in range(NZ - 1):
            total = total + self.land_1[d].astype(F32)
        self.low[...] = total.astype(BF16)
        self.start(2)

    def result(self):
        self.arrived(2)
        total = self.low[...].astype(F32)
        for d in range(NY - 1):
            total = total + self.land_2[d].astype(F32)
        result = total[0:4]
        for other in range(1, NY):
            part = total[4 * other : 4 * other + 4]
            result = jnp.where(self.place[2] == other, part, result)
        return result

    def finish(self):
        for phase in range(3):
            for one in self.copies(phase):
                one.wait_send()


def reduce_scratch(columns):
    return [
        pltpu.VMEM((NX - 1, NZ, 16, columns), BF16),
        pltpu.VMEM((NZ, 16, columns), BF16),
        pltpu.VMEM((NZ - 1, 16, columns), BF16),
        pltpu.VMEM((16, columns), BF16),
        pltpu.VMEM((NY - 1, 16, columns), BF16),
        pltpu.SemaphoreType.DMA((NX + NY + NZ - 3,)),
        pltpu.SemaphoreType.DMA((NX + NY + NZ - 3,)),
    ]


SCRATCH = dict(
    out_p=((PAIRS, 16, D // 2), BF16),
    out_c=((PAIRS, 16, D // 2), BF16),
    land_p=((2, PAIRS, 16, D // 2), BF16),
    land_c=((2, PAIRS, 16, D // 2), BF16),
    rows=((PATCH, D), BF16),
    upstream=((PATCH, D), BF16),
    bias=((16, PATCH), BF16),
    normed=((PATCH, D), BF16),
    qkv=((3, HEADS, HEAD_DIM, PATCH), BF16),
    attended=((HEADS, HEAD_DIM, PATCH), BF16),
    lse=((HEADS, 8, PATCH), F32),
    snd1=((PATCH, D), BF16),
    rcv1=((PATCH, D), BF16),
    snd2=((PATCH // 2, D), BF16),
    rcv2=((PATCH // 2, D), BF16),
    own2=((PATCH // 2, D), BF16),
    snd3=((PATCH, D), BF16),
    rcv3=((PATCH, D), BF16),
    mixed=((PATCH, D), F32),
    normed_mid=((PATCH, D), BF16),
    inverse=((PATCH, 128), F32),
    act=((PATCH, FF), BF16),
    d_pre=((PATCH, FF), BF16),
    d_mixed=((PATCH, D), BF16),
    permuted=((PATCH, D), BF16),
    d_attended=((HEADS, HEAD_DIM, PATCH), BF16),
    block=((PAIRS, 16, D // 2), BF16),
    d_qkv=((3, HEADS, HEAD_DIM, PATCH), BF16),
    grad_a=((NZ, NX, 16, AW), BF16),
    grad_b=((NY, NZ, 16, BW), BF16),
    grad_qa=((NZ, NX, 16, QA), BF16),
    grad_qb=((NZ, NX, 16, QB), BF16),
)
SEMAPHORES = dict(pair_send=(6,), pair_recv=(6,), core_send=(3, 4), core_recv=(3, 4))
INPUTS = ("points", "cotangent", "patch", "weight", "proj", "fc1", "fc2")
OUTPUTS = ("land", "slot_out", "sums_a", "sums_b", "sums_qa", "sums_qb")


def block_kernel(*refs):
    names = (*INPUTS, *OUTPUTS, *SCRATCH, *SEMAPHORES)
    ref = types.SimpleNamespace(**dict(zip(names, refs)))
    rest = refs[len(names) :]
    me, core = lax.axis_index("dp"), lax.axis_index("mp")
    parts = [
        ReduceScatter(me, core, first, grad, rest[7 * i : 7 * i + 7])
        for i, (first, grad) in enumerate(
            ((True, ref.grad_a), (False, ref.grad_b), (True, ref.grad_qa), (True, ref.grad_qb))
        )
    ]
    part_a, part_b, part_qa, part_qb = parts
    others = [p for axis in part_a.peers for p in axis[1:]]
    upstream_arrived, finish_attend = dispatch_and_attend(me, core, ref, others)
    finish_feed = feed_forward(me, core, ref, upstream_arrived, part_a, part_b)
    land, block, d_qkv = ref.land, ref.block, ref.d_qkv
    send, recv = ref.pair_send, ref.pair_recv
    pair_sends(me, core, block, land, send.at[4], recv.at[4])
    swap = to_sibling(me, core, land, send.at[5], recv.at[5])
    finish_attend()
    mask = ref.bias[...]

    def project(first, last, out):
        rows = (last - first) * HEAD_DIM
        heads = [d_qkv[j, first:last].reshape(rows, PATCH) for j in range(3)]
        grad = dot(jnp.concatenate(heads, axis=0), ref.normed[...], NN)
        out[...] = grad.T.astype(BF16).reshape(out.shape)

    def pair(i, carry):
        @pl.when(i == 5)
        def _():
            part_a.second()
            part_b.second()

        @pl.when(i == FIRST_HEADS // 2)
        def _():
            project(0, FIRST_HEADS, ref.grad_qa)
            part_qa.start()
            pair_arrived(core, land, recv.at[4])
            swap.start()

        for u in range(2):
            h = 2 * i + u
            d_query, d_key, d_value = backward_head(
                ref.qkv[0, h], ref.qkv[1, h], ref.qkv[2, h], mask,
                ref.attended[h], ref.d_attended[h], ref.lse[h][0:1],
            )
            d_qkv[0, h] = d_query
            d_qkv[1, h] = d_key
            d_qkv[2, h] = d_value
        return carry

    lax.fori_loop(0, HEADS // 2, pair, 0)
    project(FIRST_HEADS, HEADS, ref.grad_qb)
    part_qb.start()
    part_a.third()
    part_b.third()
    part_qa.second()
    part_qb.second()
    ref.sums_a[...] = part_a.result()
    ref.sums_b[...] = part_b.result()
    part_qa.third()
    part_qb.third()
    sibling_arrived(core, land, recv.at[5])
    swap.wait_send()
    pair_sent(core, block, send.at[4])
    finish_feed()
    ref.sums_qa[...] = part_qa.result()
    ref.sums_qb[...] = part_qb.result()
    for part in parts:
        part.finish()


def whole_block(*given):
    return pl.pallas_call(
        block_kernel,
        out_shape=(
            jax.ShapeDtypeStruct((2, PAIRS, 16, D // 2), BF16),
            jax.ShapeDtypeStruct((8, ROWS), jnp.int32),
            jax.ShapeDtypeStruct((4, AW), F32),
            jax.ShapeDtypeStruct((4, BW), F32),
            jax.ShapeDtypeStruct((4, QA), F32),
            jax.ShapeDtypeStruct((4, QB), F32),
        ),
        in_specs=[VMEM] * len(INPUTS),
        out_specs=(VMEM,) * len(OUTPUTS),
        scratch_shapes=[
            *(pltpu.VMEM(*shape) for shape in SCRATCH.values()),
            *(pltpu.SemaphoreType.DMA(shape) for shape in SEMAPHORES.values()),
            *reduce_scratch(AW),
            *reduce_scratch(BW),
            *reduce_scratch(QA),
            *reduce_scratch(QB),
        ],
        compiler_params=params(collective_id=1, has_side_effects=True),
        name="block",
    )(*given)


def finish_kernel(
    land, slot, sums_a, sums_b, sums_qa, sums_qb, rows_out, qkv_out, proj_out, fc1_out, fc2_out
):
    total = None
    for half in range(2):
        place = lax.broadcasted_iota(jnp.int32, (PATCH // 2, ROWS), 0) + half * (PATCH // 2)
        chosen = (place == slot[0:1, :]).astype(BF16)
        part = dot(chosen, unpack(land[half]).astype(BF16), TN)
        total = part if total is None else total + part
    rows_out[...] = total.astype(BF16)

    fc1_out[...] = sums_a[:, :FF]
    proj_out[...] = sums_a[:, FF:]
    fc2_out[...] = sums_b[...]
    first, last = sums_qa[...], sums_qb[...]
    n, m = QA // 3, QB // 3
    for j in range(3):
        qkv_out[j, :, :n] = first[:, j * n : (j + 1) * n]
        qkv_out[j, :, n:] = last[:, j * m : (j + 1) * m]


def finish(*given):
    return pl.pallas_call(
        finish_kernel,
        out_shape=(
            jax.ShapeDtypeStruct((ROWS, D), BF16),
            jax.ShapeDtypeStruct((3, 4, 256), F32),
            jax.ShapeDtypeStruct((4, 256), F32),
            jax.ShapeDtypeStruct((4, FF), F32),
            jax.ShapeDtypeStruct((4, FF), F32),
        ),
        in_specs=[VMEM] * 6,
        out_specs=(VMEM,) * 5,
        compiler_params=params(),
        name="finish",
    )(*given)


def per_device(points, patch_of, qkv_weight, proj_weight, fc1_weight, fc2_weight, cotangent):
    landed = whole_block(
        points,
        cotangent,
        patch_of.reshape(1, ROWS),
        qkv_weight.transpose(1, 0, 2),
        proj_weight,
        fc1_weight,
        fc2_weight,
    )
    block_out, grad_qkv, grad_proj, grad_fc1, grad_fc2 = finish(*landed)
    return block_out, grad_qkv.transpose(1, 0, 2), grad_proj.T, grad_fc1, grad_fc2.T


def solution(mesh):
    placed = (
        P("dp", None),
        P("dp", None),
        P(None, None, "mp"),
        P("mp", None),
        P(None, "mp"),
        P("mp", None),
        P("dp", None),
    )
    return jax.shard_map(
        per_device,
        mesh=mesh,
        in_specs=placed,
        out_specs=(P("dp", None), P("dp", None, "mp"), P("mp", "dp"), P("dp", "mp"), P("mp", "dp")),
        check_vma=False,
    )
```

```python
import math
import types

import jax
import jax.numpy as jnp
from jax import lax
from jax.experimental import pallas as pl
from jax.experimental.pallas import tpu as pltpu
from jax.sharding import PartitionSpec as P

MESH = pl.DeviceIdType.MESH
F32 = jnp.float32
BF16 = jnp.bfloat16
VMEM = pl.BlockSpec(memory_space=pltpu.VMEM)

HEADS = 16
HEAD_DIM = 16
PATCH = 1024
ROWS = 512
D = 512
FF = 1024
EPS = 1e-05
GELU_C = math.sqrt(2.0 / math.pi)
EXP2_SCALE = HEAD_DIM**-0.5 * math.log2(math.e)
EMPTY = 64.0
MASKED = -1e30
NX, NY, NZ = 4, 4, 8
PAIRS = 64
SECOND = 5
FIRST_HEADS = 12
AW = 1280
BW = 1024
QA = 3 * HEAD_DIM * FIRST_HEADS
QB = 3 * HEAD_DIM * (HEADS - FIRST_HEADS)


def dot(left, right, dims):
    return lax.dot_general(left, right, (dims, ((), ())), preferred_element_type=F32)


NN = ((1,), (0,))
NT = ((1,), (1,))
TN = ((0,), (0,))


def params(**more):
    return pltpu.CompilerParams(vmem_limit_bytes=60 << 20, **more)


def normalize(values):
    center = values - jnp.mean(values, axis=-1, keepdims=True)
    inverse = lax.rsqrt(jnp.mean(center * center, axis=-1, keepdims=True) + EPS)
    return center * inverse, inverse


def split3(x):
    a = x.astype(BF16)
    r = x - a.astype(F32)
    b = r.astype(BF16)
    return a, b, (r - b.astype(F32)).astype(BF16)


def pack(rows):
    n = rows.shape[0] // 8
    pieces = rows.reshape(n, 8, D)
    return jnp.concatenate([pieces[:, :, : D // 2], pieces[:, :, D // 2 :]], axis=1).astype(BF16)


def unpack(pieces):
    wide = pieces.astype(F32)
    n = wide.shape[0]
    return jnp.concatenate([wide[:, :8], wide[:, 8:]], axis=2).reshape(8 * n, D)


def pair_greet(me, core, extra=()):
    barrier = pltpu.get_barrier_semaphore()
    parity = lax.rem(core + me, 2)

    def greet(i, carry):
        other = 2 * lax.rem(lax.div(me, 2) + i, PAIRS) + parity
        pl.semaphore_signal(barrier, inc=1, device_id=(other, core), device_id_type=MESH)
        return carry

    lax.fori_loop(1, PAIRS, greet, 0)

    @pl.when(core == 1)
    def _():
        other = 2 * lax.div(me, 2) + parity
        pl.semaphore_signal(barrier, inc=1, device_id=(other, core), device_id_type=MESH)

    pl.semaphore_signal(barrier, inc=1, device_id=(me, 1 - core), device_id_type=MESH)
    for other in extra:
        pl.semaphore_signal(barrier, inc=1, device_id=(other, core), device_id_type=MESH)


def pair_greeted(core, extra=()):
    pl.semaphore_wait(pltpu.get_barrier_semaphore(), PAIRS + core + len(extra))


def offset(i):
    return lax.rem(i * 11, PAIRS)


def pair_sends(me, core, out, landing, send_sem, recv_sems, back=False):
    parity = lax.rem(core + me, 2)
    mine = lax.div(me, 2)

    def push(i, recv_sem):
        distance = PAIRS - offset(i) if back else offset(i)
        place = lax.rem(mine + distance, PAIRS)
        pltpu.make_async_remote_copy(
            src_ref=out.at[i if back else place],
            dst_ref=landing.at[core, mine if back else i],
            send_sem=send_sem,
            recv_sem=recv_sem,
            device_id=(2 * place + parity, core),
            device_id_type=MESH,
        ).start()

    @pl.when(core == 0)
    def _():
        own = landing.at[core, mine if back else 0]
        pltpu.make_async_copy(out.at[0 if back else mine], own, recv_sems[0]).start()

    @pl.when(core == 1)
    def _():
        push(0, recv_sems[0])

    each = PAIRS // len(recv_sems)
    for k, recv_sem in enumerate(recv_sems):

        def step(i, carry, recv_sem=recv_sem):
            push(i, recv_sem)
            return carry

        lax.fori_loop(max(1, k * each), (k + 1) * each, step, 0)


def pair_arrived(landed, recv_sem):
    pltpu.make_async_copy(landed, landed, recv_sem).wait()


def pair_sent(core, out, send_sem):
    most = out.at[pl.ds(0, PAIRS - 1)]
    pltpu.make_async_copy(most, most, send_sem).wait()

    @pl.when(core == 1)
    def _():
        pltpu.make_async_copy(out.at[0], out.at[0], send_sem).wait()


def to_sibling(me, core, landed, send_sem, recv_sem):
    return pltpu.make_async_remote_copy(
        src_ref=landed,
        dst_ref=landed,
        send_sem=send_sem,
        recv_sem=recv_sem,
        device_id=(me, 1 - core),
        device_id_type=MESH,
    )


def slot_rows(patch, me):
    member = (lax.broadcasted_iota(jnp.int32, (128, ROWS), 0) == patch).astype(BF16)
    before = (
        lax.broadcasted_iota(jnp.int32, (ROWS, ROWS), 0)
        < lax.broadcasted_iota(jnp.int32, (ROWS, ROWS), 1)
    ).astype(BF16)
    earlier = dot(member, before, NN)
    within = jnp.sum(earlier * member.astype(F32), axis=0, keepdims=True).astype(jnp.int32)
    return ((patch + me) & 1) * (PATCH // 2) + (patch >> 1) * 8 + within


def forward_head(query, key, value, bias):
    scaled = split3(query.astype(F32) * EXP2_SCALE)
    wide_query = jnp.concatenate([*scaled, jnp.ones((16, PATCH), BF16)], axis=0)
    wide_key = jnp.concatenate([key, key, key, bias], axis=0)
    scores = dot(wide_key, wide_query, TN)
    maxima = jnp.max(scores, axis=0, keepdims=True)
    weights = jnp.exp2(scores - maxima)
    totals = jnp.sum(weights, axis=0, keepdims=True)
    result = dot(value, weights.astype(BF16), NN) / totals
    return result.astype(BF16), maxima + jnp.log2(totals)


def dispatch_and_attend(me, core, ref, others):
    for load in ref.loads:
        load.start()
    pair_greet(me, core, others)
    slot = slot_rows(ref.patch[...], me)
    place = lax.broadcasted_iota(jnp.int32, (PATCH // 2, ROWS), 0) + core * (PATCH // 2)
    chosen = (place == slot).astype(BF16)
    filled = dot(chosen, jnp.ones((ROWS, 128), BF16), NN)
    fill = EMPTY * (1.0 - jnp.concatenate([filled] * (D // 128), axis=1))
    ref.out_p[...] = pack(dot(chosen, ref.points[...], NN) + fill)
    pair_greeted(core, others)
    send, recv = ref.pair_send, ref.pair_recv
    pair_sends(me, core, ref.out_p, ref.land_p, send.at[0], (recv.at[0], recv.at[6]))
    ref.out_c[...] = pack(dot(chosen, ref.cotangent[...], NN))
    ref.order_b[...] = row_order(lambda y, z, x: (y, z, x), (NY, NZ, NX))
    ref.order_q[...] = row_order(lambda x, y, z: (y, z, x), (NX, NY, NZ))

    def landed(half, part):
        return ref.land_p.at[half, pl.ds(part * 32, 32)]

    swaps = [
        to_sibling(me, core, landed(core, part), send.at[2 + 4 * part], recv.at[2 + 5 * part])
        for part in range(2)
    ]
    swap_c = to_sibling(me, core, ref.land_c.at[core], send.at[3], recv.at[3])
    ones = jnp.ones((16, 128), BF16)

    def receive(half, part):
        start = pl.multiple_of(half * 512 + part * 256, 256)
        at = pl.ds(start, 256)
        wide = unpack(ref.land_p[half, part * 32 : part * 32 + 32])
        empty = wide > 0.5 * EMPTY
        real = jnp.where(empty, 0.0, wide)
        ref.rows[at, :] = real.astype(BF16)
        count = dot(ones, jnp.where(empty[:, :128], 1.0, 0.0).astype(BF16), NT)
        first_row = lax.broadcasted_iota(jnp.int32, (16, 256), 0) == 0
        ref.bias[:, at] = jnp.where(first_row & (count > 0.5), MASKED, 0.0).astype(BF16)
        normed = normalize(real)[0].astype(BF16)
        ref.normed[at, :] = normed
        for j in range(3):
            projected = dot(ref.weight[j], normed, ((0,), (1,))).astype(BF16)
            ref.qkv[j, :, :, at] = projected.reshape(HEADS, HEAD_DIM, 256)

    for load in ref.loads:
        load.wait()
    pair_arrived(landed(core, 0), recv.at[0])
    swaps[0].start()
    receive(core, 0)
    pair_sends(me, core, ref.out_c, ref.land_c, send.at[1], (recv.at[1],))
    pair_arrived(landed(core, 1), recv.at[6])
    swaps[1].start()
    receive(core, 1)
    for part in range(2):
        pair_arrived(landed(1 - core, part), recv.at[2 + 5 * part])
        receive(1 - core, part)
    mask = ref.bias[...]

    def pair(i, carry):
        @pl.when(i == 6)
        def _():
            pair_arrived(ref.land_c.at[core], recv.at[1])
            swap_c.start()

        for u in range(2):
            h = 2 * i + u
            result, lse = forward_head(ref.qkv[0, h], ref.qkv[1, h], ref.qkv[2, h], mask)
            ref.attended[h] = result
            ref.lse[h] = jnp.broadcast_to(lse, (8, PATCH))
        return carry

    lax.fori_loop(0, HEADS // 2, pair, 0)

    def upstream_arrived():
        pair_arrived(ref.land_c.at[1 - core], recv.at[3])
        for half in range(2):
            for part in range(2):
                at = half * 512 + part * 256
                pieces = ref.land_c[half, part * 32 : part * 32 + 32]
                ref.upstream[at : at + 256, :] = unpack(pieces).astype(BF16)
        ref.permuted[...] = dot(ref.upstream[...], ref.order_b[...], NN).astype(BF16)

    def finish():
        for swap in (*swaps, swap_c):
            swap.wait_send()
        pair_sent(core, ref.out_p, send.at[0])
        pair_sent(core, ref.out_c, send.at[1])

    return slot, upstream_arrived, finish


def backward_head(query, key, value, bias, attended, upstream, lse):
    shape = (16, PATCH)
    row = lax.broadcasted_iota(jnp.int32, shape, 0)
    one = jnp.ones(shape, BF16)
    zero = jnp.zeros(shape, BF16)

    def stacked(*given):
        total = zero
        for at, value_at in enumerate(given):
            total = jnp.where(row == at, value_at, total)
        return total

    lse_pieces = split3(-jnp.broadcast_to(lse, shape))
    scaled = split3(query.astype(F32) * EXP2_SCALE)
    wide_query = jnp.concatenate([*scaled, stacked(one, *lse_pieces)], axis=0)
    wide_key = jnp.concatenate([key, key, key, stacked(bias, one, one, one)], axis=0)
    scale = HEAD_DIM**-0.5
    upstream_wide = upstream.astype(F32)
    delta = -scale * jnp.sum(upstream_wide * attended.astype(F32), axis=0, keepdims=True)
    delta_pieces = split3(jnp.broadcast_to(delta, shape))
    wide_upstream = jnp.concatenate(
        [(scale * upstream_wide).astype(BF16), stacked(*delta_pieces)], axis=0
    )
    wide_value = jnp.concatenate([value, stacked(one, one, one)], axis=0)
    d_query, d_key, d_value = [], None, None
    for part in range(2):
        at = slice(part * 512, part * 512 + 512)
        weights = jnp.exp2(dot(wide_query[:, at], wide_key, TN))
        d_scores = (weights * dot(wide_upstream[:, at], wide_value, TN)).astype(BF16)
        d_query.append(dot(key, d_scores, NT))
        more_key = dot(query[:, at], d_scores, NN)
        more_value = dot(upstream[:, at], weights.astype(BF16), NN)
        d_key = more_key if d_key is None else d_key + more_key
        d_value = more_value if d_value is None else d_value + more_value
    return jnp.concatenate(d_query, axis=1).astype(BF16), d_key.astype(BF16), d_value.astype(BF16)


def gelu_both(values):
    squared = values * values
    tangent = jnp.tanh(GELU_C * (values + 0.044715 * squared * values))
    half = 0.5 * (1.0 + tangent)
    derivative = half + 0.5 * values * (1.0 - tangent * tangent) * GELU_C * (
        1.0 + 3.0 * 0.044715 * squared
    )
    return values * half, derivative


CHUNK = 512


def row_order(to_yzx, sizes):
    place = lax.broadcasted_iota(jnp.int32, (D, D), 1)
    rest, parts = place >> 2, []
    for size in reversed(sizes):
        parts.insert(0, rest & (size - 1))
        rest = rest >> (size.bit_length() - 1)
    y, z, x = to_yzx(*parts)
    channel = (z << 6) + (x << 4) + (y << 2) + (place & 3)
    return (lax.broadcasted_iota(jnp.int32, (D, D), 0) == channel).astype(BF16)


def feed_forward(me, core, ref, upstream_arrived, part_a, part_b):
    sibling = (me, 1 - core)
    chunks = PATCH // CHUNK
    half = chunks // 2
    proj, fc1, fc2 = ref.proj, ref.fc1, ref.fc2

    def place(i):
        return lax.rem(i + half * (1 - core), chunks)

    def span(k):
        return pl.ds(pl.multiple_of(k * CHUNK, CHUNK), CHUNK)

    def copy(kind, i, src, dst):
        return pltpu.make_async_remote_copy(
            src_ref=src,
            dst_ref=dst,
            send_sem=ref.core_send.at[kind, i],
            recv_sem=ref.core_recv.at[kind, i],
            device_id=sibling,
            device_id_type=MESH,
        )

    def copy1(k):
        return copy(0, k, ref.snd1.at[span(k), :], ref.rcv1.at[span(k), :])

    def copy2(i):
        at = pl.ds(i * CHUNK, CHUNK)
        return copy(1, i, ref.snd2.at[at, :], ref.rcv2.at[at, :])

    def copy3(k):
        return copy(2, k, ref.snd3.at[span(k), :], ref.rcv3.at[span(k), :])

    for i in range(chunks):
        k = place(i)
        heads = ref.attended[:, :, span(k)].reshape(256, CHUNK)
        ref.snd1[span(k), :] = dot(heads, proj[...], TN).astype(BF16)
        copy1(k).start()
    upstream_arrived()

    for i in range(chunks):
        k = place(i)
        at = span(k)
        copy1(k).wait_recv()
        added = ref.snd1[at, :].astype(F32) + ref.rcv1[at, :].astype(F32)
        total = ref.rows[at, :].astype(F32) + added
        ref.mixed[at, :] = total
        normed, inv = normalize(total)
        ref.inverse[at, :] = jnp.broadcast_to(inv, (CHUNK, 128))
        low = normed.astype(BF16)
        ref.normed_mid[at, :] = low
        activation, derivative = gelu_both(dot(low, fc1[...], NN))
        act_low = activation.astype(BF16)
        ref.act[at, :] = act_low
        partial = dot(act_low, fc2[...], NN).astype(BF16)
        if i < half:
            ref.snd2[i * CHUNK : (i + 1) * CHUNK, :] = partial
            copy2(i).start()
        else:
            ref.own2[(i - half) * CHUNK : (i - half + 1) * CHUNK, :] = partial
        d_low = (dot(ref.upstream[at, :], fc2[...], NT) * derivative).astype(BF16)
        ref.d_pre[at, :] = d_low
        ref.snd3[at, :] = dot(d_low, fc1[...], NT).astype(BF16)
        copy3(k).start()

    for part in range(4):
        cols = slice(part * 256, part * 256 + 256)
        grad = dot(ref.permuted[...], ref.act[:, cols], TN).astype(BF16)
        ref.grad_b[:, :, :, cols] = grad.reshape(NY, NZ, 16, 256)
    part_b.start()
    for part in range(4):
        cols = slice(part * 256, part * 256 + 256)
        grad = dot(ref.normed_mid[...], ref.d_pre[:, cols], TN).astype(BF16)
        ref.grad_a[:, :, :, cols] = grad.reshape(NZ, NX, 16, 256)

    for i in range(chunks):
        k = place(i)
        at = span(k)
        copy3(k).wait_recv()
        back = ref.snd3[at, :].astype(F32) + ref.rcv3[at, :].astype(F32)
        inv = ref.inverse[at, :][:, 0:1]
        total = ref.mixed[at, :]
        center = total - jnp.mean(total, axis=-1, keepdims=True)
        normed = center * inv
        mean_grad = jnp.mean(back, axis=-1, keepdims=True)
        mean_mixed = jnp.mean(back * normed, axis=-1, keepdims=True)
        through = inv * (back - mean_grad - normed * mean_mixed)
        low = (ref.upstream[at, :].astype(F32) + through).astype(BF16)
        ref.d_mixed[at, :] = low
        heads = dot(proj[...], low, NT).astype(BF16)
        ref.d_attended[:, :, at] = heads.reshape(HEADS, HEAD_DIM, CHUNK)

    grad = dot(ref.attended[...].reshape(256, PATCH), ref.d_mixed[...], NN).T.astype(BF16)
    ref.grad_a[:, :, :, FF:AW] = grad.reshape(NZ, NX, 16, AW - FF)
    part_a.start()

    for i in range(half):
        copy2(i).wait_recv()
        own = slice(i * CHUNK, (i + 1) * CHUNK)
        added = ref.own2[own, :].astype(F32) + ref.rcv2[own, :].astype(F32)
        total = ref.mixed[span(place(i + half)), :] + added
        ref.block[i * CHUNK // 8 : (i + 1) * CHUNK // 8] = pack(total.astype(BF16).astype(F32))

    def finish():
        for k in range(chunks):
            copy1(k).wait_send()
            copy3(k).wait_send()
        for i in range(half):
            copy2(i).wait_send()

    return finish


class ReduceScatter:
    def __init__(self, me, core, x_first, grad, scratch):
        z, x, y = lax.div(me, NX * NY), lax.rem(lax.div(me, NY), NX), lax.rem(me, NY)
        at_x = [(z * NX + lax.rem(x + d, NX)) * NY + y for d in range(NX)]
        at_z = [(lax.rem(z + d, NZ) * NX + x) * NY + y for d in range(NZ)]
        at_y = [(z * NX + x) * NY + lax.rem(y + d, NY) for d in range(NY)]
        self.core, self.x_first = core, x_first
        self.peers = (at_x, at_z, at_y) if x_first else (at_y, at_z, at_x)
        self.place = (x, z, y) if x_first else (y, z, x)
        self.grad = grad
        self.land_0, self.mid, self.land_1, self.low, self.land_2, self.send, self.recv = scratch

    def copy(self, phase, d, src, dst):
        base = (0, NX - 1, NX + NZ - 2)[phase]
        return pltpu.make_async_remote_copy(
            src_ref=src,
            dst_ref=dst,
            send_sem=self.send.at[base + d - 1],
            recv_sem=self.recv.at[base + d - 1],
            device_id=(self.peers[phase][d], self.core),
            device_id_type=MESH,
        )

    def piece(self, d):
        at = lax.rem(self.place[0] + d, NX)
        return self.grad.at[:, at] if self.x_first else self.grad.at[at]

    def copies(self, phase):
        if phase == 0:
            return [self.copy(0, d, self.piece(d), self.land_0.at[d - 1]) for d in range(1, NX)]
        if phase == 1:
            z = self.place[1]
            return [
                self.copy(1, d, self.mid.at[lax.rem(z + d, NZ)], self.land_1.at[d - 1])
                for d in range(1, NZ)
            ]
        return [self.copy(2, d, self.low, self.land_2.at[d - 1]) for d in range(1, NY)]

    def start(self, phase=0):
        for one in self.copies(phase):
            one.start()

    def arrived(self, phase):
        for one in self.copies(phase):
            one.wait_recv()

    def second(self):
        self.arrived(0)
        mine = self.place[0]

        def step(i, carry):
            own = self.grad[i, mine] if self.x_first else self.grad[mine, i]
            total = own.astype(F32)
            for d in range(NX - 1):
                total = total + self.land_0[d, i].astype(F32)
            self.mid[i] = total.astype(BF16)
            return carry

        lax.fori_loop(0, NZ, step, 0)
        self.start(1)

    def third(self):
        self.arrived(1)
        total = self.mid[self.place[1]].astype(F32)
        for d in range(NZ - 1):
            total = total + self.land_1[d].astype(F32)
        self.low[...] = total.astype(BF16)
        self.start(2)

    def result(self):
        self.arrived(2)
        total = self.low[...].astype(F32)
        for d in range(NY - 1):
            total = total + self.land_2[d].astype(F32)
        result = total[0:4]
        for other in range(1, NY):
            part = total[4 * other : 4 * other + 4]
            result = jnp.where(self.place[2] == other, part, result)
        return result

    def finish(self):
        for phase in range(3):
            for one in self.copies(phase):
                one.wait_send()


class PlaneReduceScatter:
    def __init__(self, me, core, grad, scratch):
        z, x, y = lax.div(me, NX * NY), lax.rem(lax.div(me, NY), NX), lax.rem(me, NY)
        self.core, self.grad, self.place = core, grad, (z, x, y)
        self.land_0, self.mid, self.land_1, self.send, self.recv = scratch
        at = [(lax.rem(x + d // NY, NX), lax.rem(y + d % NY, NY)) for d in range(NX * NY)]
        self.plane = [((z * NX + x2) * NY + y2, x2, y2) for x2, y2 in at]
        other_z = [lax.rem(z + d, NZ) for d in range(NZ)]
        self.line = [((z2 * NX + x) * NY + y, z2) for z2 in other_z]

    def copy(self, k, src, dst, peer):
        return pltpu.make_async_remote_copy(
            src_ref=src,
            dst_ref=dst,
            send_sem=self.send.at[k],
            recv_sem=self.recv.at[k],
            device_id=(peer, self.core),
            device_id_type=MESH,
        )

    def group(self, z):
        return pl.ds(pl.multiple_of(lax.div(z, 4) * 16, 16), 16)

    def copies(self, phase):
        if phase == 0:
            return [
                self.copy(d - 1, self.grad.at[x, y], self.land_0.at[d - 1], peer)
                for d, (peer, x, y) in enumerate(self.plane)
                if d
            ]
        base = NX * NY - 2
        return [
            self.copy(base + d, self.mid.at[self.group(z), :], self.land_1.at[d - 1], peer)
            for d, (peer, z) in enumerate(self.line)
            if d
        ]

    def start(self):
        for one in self.copies(0):
            one.start()

    def second(self):
        for one in self.copies(0):
            one.wait_recv()
        _, x, y = self.place
        total = self.grad[x, y].astype(F32)
        for d in range(NX * NY - 1):
            total = total + self.land_0[d].astype(F32)
        self.mid[...] = total.astype(BF16)
        for one in self.copies(1):
            one.start()

    def result(self):
        for one in self.copies(1):
            one.wait_recv()
        z = self.place[0]
        total = self.mid[self.group(z), :].astype(F32)
        for d in range(NZ - 1):
            total = total + self.land_1[d].astype(F32)
        result = total[0:4]
        for other in range(1, 4):
            part = total[4 * other : 4 * other + 4]
            result = jnp.where(lax.rem(z, 4) == other, part, result)
        return result

    def finish(self):
        for phase in range(2):
            for one in self.copies(phase):
                one.wait_send()


def plane_scratch(columns):
    return [
        pltpu.VMEM((NX * NY - 1, 32, columns), BF16),
        pltpu.VMEM((32, columns), BF16),
        pltpu.VMEM((NZ - 1, 16, columns), BF16),
        pltpu.SemaphoreType.DMA((NX * NY + NZ - 2,)),
        pltpu.SemaphoreType.DMA((NX * NY + NZ - 2,)),
    ]


def reduce_scratch(columns):
    return [
        pltpu.VMEM((NX - 1, NZ, 16, columns), BF16),
        pltpu.VMEM((NZ, 16, columns), BF16),
        pltpu.VMEM((NZ - 1, 16, columns), BF16),
        pltpu.VMEM((16, columns), BF16),
        pltpu.VMEM((NY - 1, 16, columns), BF16),
        pltpu.SemaphoreType.DMA((NX + NY + NZ - 3,)),
        pltpu.SemaphoreType.DMA((NX + NY + NZ - 3,)),
    ]


SCRATCH = dict(
    out_p=((PAIRS, 16, D // 2), BF16),
    out_c=((PAIRS, 16, D // 2), BF16),
    land_p=((2, PAIRS, 16, D // 2), BF16),
    land_c=((2, PAIRS, 16, D // 2), BF16),
    rows=((PATCH, D), BF16),
    upstream=((PATCH, D), BF16),
    bias=((16, PATCH), BF16),
    normed=((PATCH, D), BF16),
    qkv=((3, HEADS, HEAD_DIM, PATCH), BF16),
    attended=((HEADS, HEAD_DIM, PATCH), BF16),
    lse=((HEADS, 8, PATCH), F32),
    snd1=((PATCH, D), BF16),
    rcv1=((PATCH, D), BF16),
    snd2=((PATCH // 2, D), BF16),
    rcv2=((PATCH // 2, D), BF16),
    own2=((PATCH // 2, D), BF16),
    snd3=((PATCH, D), BF16),
    rcv3=((PATCH, D), BF16),
    mixed=((PATCH, D), F32),
    normed_mid=((PATCH, D), BF16),
    inverse=((PATCH, 128), F32),
    act=((PATCH, FF), BF16),
    d_pre=((PATCH, FF), BF16),
    d_mixed=((PATCH, D), BF16),
    permuted=((PATCH, D), BF16),
    d_attended=((HEADS, HEAD_DIM, PATCH), BF16),
    block=((PAIRS, 16, D // 2), BF16),
    d_qkv=((3, HEADS, HEAD_DIM, PATCH), BF16),
    grad_a=((NZ, NX, 16, AW), BF16),
    grad_b=((NY, NZ, 16, BW), BF16),
    grad_qa=((NZ, NX, 16, QA), BF16),
    grad_qb=((NX, NY, 32, QB), BF16),
    land=((2, PAIRS, 16, D // 2), BF16),
    weight=((3, D, 256), BF16),
    proj=((256, D), BF16),
    fc1=((D, FF), BF16),
    fc2=((FF, D), BF16),
    order_b=((D, D), BF16),
    order_q=((D, D), BF16),
)
SEMAPHORES = dict(near=(4,), pair_send=(7,), pair_recv=(8,), core_send=(3, 4), core_recv=(3, 4))
INPUTS = ("points", "cotangent", "patch", "far_weight", "far_proj", "far_fc1", "far_fc2")
WEIGHTS = ("weight", "proj", "fc1", "fc2")
OUTPUTS = ("rows_out", "sums_a", "sums_b", "sums_qa", "sums_qb")


def block_kernel(*refs):
    names = (*INPUTS, *OUTPUTS, *SCRATCH, *SEMAPHORES)
    ref = types.SimpleNamespace(**dict(zip(names, refs)))
    rest = refs[len(names) :]
    ref.loads = [
        pltpu.make_async_copy(getattr(ref, "far_" + name), getattr(ref, name), ref.near.at[k])
        for k, name in enumerate(WEIGHTS)
    ]
    me, core = lax.axis_index("dp"), lax.axis_index("mp")
    parts = [
        ReduceScatter(me, core, first, grad, rest[7 * i : 7 * i + 7])
        for i, (first, grad) in enumerate(
            ((True, ref.grad_a), (False, ref.grad_b), (True, ref.grad_qa))
        )
    ]
    part_qb = PlaneReduceScatter(me, core, ref.grad_qb, rest[21:])
    part_a, part_b, part_qa = parts
    others = [peer for peer, *_ in (*part_qb.plane[1:], *part_qb.line[1:])]
    slot, upstream_arrived, finish_attend = dispatch_and_attend(me, core, ref, others)
    finish_feed = feed_forward(me, core, ref, upstream_arrived, part_a, part_b)
    land, block, d_qkv = ref.land, ref.block, ref.d_qkv
    send, recv = ref.pair_send, ref.pair_recv
    pair_sends(me, core, block, land, send.at[4], (recv.at[4],), back=True)
    swap = to_sibling(me, core, land.at[core], send.at[5], recv.at[5])
    finish_attend()
    mask = ref.bias[...]

    def project(first, last):
        rows = (last - first) * HEAD_DIM
        heads = [d_qkv[j, first:last].reshape(rows, PATCH) for j in range(3)]
        return dot(jnp.concatenate(heads, axis=0), ref.normed[...], NN)

    def pair(i, carry):
        @pl.when(i == SECOND)
        def _():
            part_a.second()
            part_b.second()

        @pl.when(i == FIRST_HEADS // 2)
        def _():
            grad = project(0, FIRST_HEADS).T.astype(BF16)
            ref.grad_qa[...] = grad.reshape(NZ, NX, 16, QA)
            part_qa.start()
            pair_arrived(land.at[core], recv.at[4])
            swap.start()

        for u in range(2):
            h = 2 * i + u
            d_query, d_key, d_value = backward_head(
                ref.qkv[0, h], ref.qkv[1, h], ref.qkv[2, h], mask,
                ref.attended[h], ref.d_attended[h], ref.lse[h][0:1],
            )
            d_qkv[0, h] = d_query
            d_qkv[1, h] = d_key
            d_qkv[2, h] = d_value
        return carry

    lax.fori_loop(0, HEADS // 2, pair, 0)
    grad = dot(project(FIRST_HEADS, HEADS).astype(BF16), ref.order_q[...], NN)
    ref.grad_qb[...] = grad.T.astype(BF16).reshape(NX, NY, 32, QB)
    part_qb.start()
    part_a.third()
    part_b.third()
    part_qa.second()
    part_qb.second()
    part_qa.third()
    pair_arrived(land.at[1 - core], recv.at[5])
    total = None
    for half in range(2):
        place = lax.broadcasted_iota(jnp.int32, (PATCH // 2, ROWS), 0) + half * (PATCH // 2)
        chosen = (place == slot).astype(BF16)
        part = dot(chosen, unpack(land[half]).astype(BF16), TN)
        total = part if total is None else total + part
    ref.rows_out[...] = total.astype(BF16)
    ref.sums_a[...] = part_a.result()
    ref.sums_b[...] = part_b.result()
    swap.wait_send()
    pair_sent(core, block, send.at[4])
    finish_feed()
    ref.sums_qa[...] = part_qa.result()
    ref.sums_qb[...] = part_qb.result()
    for part in (*parts, part_qb):
        part.finish()


def whole_block(*given):
    return pl.pallas_call(
        block_kernel,
        out_shape=(
            jax.ShapeDtypeStruct((ROWS, D), BF16),
            jax.ShapeDtypeStruct((4, AW), F32),
            jax.ShapeDtypeStruct((4, BW), F32),
            jax.ShapeDtypeStruct((4, QA), F32),
            jax.ShapeDtypeStruct((4, QB), F32),
        ),
        in_specs=[VMEM] * 3 + [pl.BlockSpec(memory_space=pl.ANY)] * len(WEIGHTS),
        out_specs=(VMEM,) * len(OUTPUTS),
        scratch_shapes=[
            *(pltpu.VMEM(*shape) for shape in SCRATCH.values()),
            *(pltpu.SemaphoreType.DMA(shape) for shape in SEMAPHORES.values()),
            *reduce_scratch(AW),
            *reduce_scratch(BW),
            *reduce_scratch(QA),
            *plane_scratch(QB),
        ],
        compiler_params=params(collective_id=1, has_side_effects=True),
        name="block",
    )(*given)


def finish_kernel(
    rows, sums_a, sums_b, sums_qa, sums_qb, rows_out, qkv_out, proj_out, fc1_out, fc2_out
):
    rows_out[...] = rows[...]
    fc1_out[...] = sums_a[:, :FF]
    proj_out[...] = sums_a[:, FF:]
    fc2_out[...] = sums_b[...]
    first, last = sums_qa[...], sums_qb[...]
    n, m = QA // 3, QB // 3
    for j in range(3):
        qkv_out[j, :, :n] = first[:, j * n : (j + 1) * n]
        qkv_out[j, :, n:] = last[:, j * m : (j + 1) * m]


def finish(*given):
    return pl.pallas_call(
        finish_kernel,
        out_shape=(
            jax.ShapeDtypeStruct((ROWS, D), BF16),
            jax.ShapeDtypeStruct((3, 4, 256), F32),
            jax.ShapeDtypeStruct((4, 256), F32),
            jax.ShapeDtypeStruct((4, FF), F32),
            jax.ShapeDtypeStruct((4, FF), F32),
        ),
        in_specs=[VMEM] * 5,
        out_specs=(VMEM,) * 5,
        compiler_params=params(),
        name="finish",
    )(*given)


def per_device(points, patch_of, qkv_weight, proj_weight, fc1_weight, fc2_weight, cotangent):
    landed = whole_block(
        points,
        cotangent,
        patch_of.reshape(1, ROWS),
        qkv_weight.transpose(1, 0, 2),
        proj_weight,
        fc1_weight,
        fc2_weight,
    )
    block_out, grad_qkv, grad_proj, grad_fc1, grad_fc2 = finish(*landed)
    return block_out, grad_qkv.transpose(1, 0, 2), grad_proj.T, grad_fc1, grad_fc2.T


def solution(mesh):
    placed = (
        P("dp", None),
        P("dp", None),
        P(None, None, "mp"),
        P("mp", None),
        P(None, "mp"),
        P("mp", None),
        P("dp", None),
    )
    return jax.shard_map(
        per_device,
        mesh=mesh,
        in_specs=placed,
        out_specs=(P("dp", None), P("dp", None, "mp"), P("mp", "dp"), P("dp", "mp"), P("mp", "dp")),
        check_vma=False,
    )
```

```python
import math
import types

import jax
import jax.numpy as jnp
from jax import lax
from jax.experimental import pallas as pl
from jax.experimental.pallas import tpu as pltpu
from jax.sharding import PartitionSpec as P

MESH = pl.DeviceIdType.MESH
F32 = jnp.float32
BF16 = jnp.bfloat16
VMEM = pl.BlockSpec(memory_space=pltpu.VMEM)

HEADS = 16
HEAD_DIM = 16
PATCH = 1024
ROWS = 512
D = 512
FF = 1024
EPS = 1e-05
GELU_C = math.sqrt(2.0 / math.pi)
EXP2_SCALE = HEAD_DIM**-0.5 * math.log2(math.e)
EMPTY = 64.0
MASKED = -1e30
NX, NY, NZ = 4, 4, 8
PAIRS = 64
SECOND = 5
FIRST_HEADS = 12
AW = 1280
BW = 1024
QA = 3 * HEAD_DIM * FIRST_HEADS
QB = 3 * HEAD_DIM * (HEADS - FIRST_HEADS)


def dot(left, right, dims):
    return lax.dot_general(left, right, (dims, ((), ())), preferred_element_type=F32)


NN = ((1,), (0,))
NT = ((1,), (1,))
TN = ((0,), (0,))


def params(**more):
    return pltpu.CompilerParams(vmem_limit_bytes=60 << 20, **more)


def normalize(values):
    center = values - jnp.mean(values, axis=-1, keepdims=True)
    inverse = lax.rsqrt(jnp.mean(center * center, axis=-1, keepdims=True) + EPS)
    return center * inverse, inverse


def split3(x):
    a = x.astype(BF16)
    r = x - a.astype(F32)
    b = r.astype(BF16)
    return a, b, (r - b.astype(F32)).astype(BF16)


def pack(rows):
    n = rows.shape[0] // 8
    pieces = rows.reshape(n, 8, D)
    return jnp.concatenate([pieces[:, :, : D // 2], pieces[:, :, D // 2 :]], axis=1).astype(BF16)


def unpack(pieces):
    wide = pieces.astype(F32)
    n = wide.shape[0]
    return jnp.concatenate([wide[:, :8], wide[:, 8:]], axis=2).reshape(8 * n, D)


def pair_greet(me, core, extra=()):
    barrier = pltpu.get_barrier_semaphore()
    parity = lax.rem(core + me, 2)

    def greet(i, carry):
        other = 2 * lax.rem(lax.div(me, 2) + i, PAIRS) + parity
        pl.semaphore_signal(barrier, inc=1, device_id=(other, core), device_id_type=MESH)
        return carry

    lax.fori_loop(1, PAIRS, greet, 0)

    @pl.when(core == 1)
    def _():
        other = 2 * lax.div(me, 2) + parity
        pl.semaphore_signal(barrier, inc=1, device_id=(other, core), device_id_type=MESH)

    pl.semaphore_signal(barrier, inc=1, device_id=(me, 1 - core), device_id_type=MESH)
    for other in extra:
        pl.semaphore_signal(barrier, inc=1, device_id=(other, core), device_id_type=MESH)


def pair_greeted(core, extra=()):
    pl.semaphore_wait(pltpu.get_barrier_semaphore(), PAIRS + core + len(extra))


def offset(i):
    return lax.rem(i * 11, PAIRS)


def pair_sends(me, core, out, landing, send_sem, recv_sems, back=False):
    parity = lax.rem(core + me, 2)
    mine = lax.div(me, 2)

    def push(i, recv_sem):
        distance = PAIRS - offset(i) if back else offset(i)
        place = lax.rem(mine + distance, PAIRS)
        pltpu.make_async_remote_copy(
            src_ref=out.at[i if back else place],
            dst_ref=landing.at[core, mine if back else i],
            send_sem=send_sem,
            recv_sem=recv_sem,
            device_id=(2 * place + parity, core),
            device_id_type=MESH,
        ).start()

    @pl.when(core == 0)
    def _():
        own = landing.at[core, mine if back else 0]
        pltpu.make_async_copy(out.at[0 if back else mine], own, recv_sems[0]).start()

    @pl.when(core == 1)
    def _():
        push(0, recv_sems[0])

    each = PAIRS // len(recv_sems)
    for k, recv_sem in enumerate(recv_sems):

        def step(i, carry, recv_sem=recv_sem):
            push(i, recv_sem)
            return carry

        lax.fori_loop(max(1, k * each), (k + 1) * each, step, 0)


def pair_arrived(landed, recv_sem):
    pltpu.make_async_copy(landed, landed, recv_sem).wait()


def pair_sent(core, out, send_sem):
    most = out.at[pl.ds(0, PAIRS - 1)]
    pltpu.make_async_copy(most, most, send_sem).wait()

    @pl.when(core == 1)
    def _():
        pltpu.make_async_copy(out.at[0], out.at[0], send_sem).wait()


def to_sibling(me, core, landed, send_sem, recv_sem):
    return pltpu.make_async_remote_copy(
        src_ref=landed,
        dst_ref=landed,
        send_sem=send_sem,
        recv_sem=recv_sem,
        device_id=(me, 1 - core),
        device_id_type=MESH,
    )


def slot_rows(patch, me):
    member = (lax.broadcasted_iota(jnp.int32, (128, ROWS), 0) == patch).astype(BF16)
    before = (
        lax.broadcasted_iota(jnp.int32, (ROWS, ROWS), 0)
        < lax.broadcasted_iota(jnp.int32, (ROWS, ROWS), 1)
    ).astype(BF16)
    earlier = dot(member, before, NN)
    within = jnp.sum(earlier * member.astype(F32), axis=0, keepdims=True).astype(jnp.int32)
    return ((patch + me) & 1) * (PATCH // 2) + (patch >> 1) * 8 + within


def forward_head(query, key, value, bias):
    scaled = split3(query.astype(F32) * EXP2_SCALE)
    wide_query = jnp.concatenate([*scaled, jnp.ones((16, PATCH), BF16)], axis=0)
    wide_key = jnp.concatenate([key, key, key, bias], axis=0)
    scores = dot(wide_key, wide_query, TN)
    maxima = jnp.max(scores, axis=0, keepdims=True)
    weights = jnp.exp2(scores - maxima)
    totals = jnp.sum(weights, axis=0, keepdims=True)
    result = dot(value, weights.astype(BF16), NN) / totals
    return result.astype(BF16), maxima + jnp.log2(totals)


def dispatch_and_attend(me, core, ref, others):
    for load in ref.loads:
        load.start()
    pair_greet(me, core, others)
    for load in ref.loads[:3]:
        load.wait()
    slot = slot_rows(ref.patch[...], me)
    place = lax.broadcasted_iota(jnp.int32, (PATCH // 2, ROWS), 0) + core * (PATCH // 2)
    chosen = (place == slot).astype(BF16)
    filled = dot(chosen, jnp.ones((ROWS, 128), BF16), NN)
    fill = EMPTY * (1.0 - jnp.concatenate([filled] * (D // 128), axis=1))
    ref.out_p[...] = pack(dot(chosen, ref.points[...], NN) + fill)
    pair_greeted(core, others)
    send, recv = ref.pair_send, ref.pair_recv
    pair_sends(me, core, ref.out_p, ref.land_p, send.at[0], (recv.at[0], recv.at[6]))
    ref.out_c[...] = pack(dot(chosen, ref.cotangent[...], NN))
    ref.order_b[...] = row_order(lambda y, z, x: (y, z, x), (NY, NZ, NX))
    ref.order_q[...] = row_order(lambda x, y, z: (y, z, x), (NX, NY, NZ))

    def landed(half, part):
        return ref.land_p.at[half, pl.ds(part * 32, 32)]

    swaps = [
        to_sibling(me, core, landed(core, part), send.at[2 + 4 * part], recv.at[2 + 5 * part])
        for part in range(2)
    ]
    swap_c = to_sibling(me, core, ref.land_c.at[core], send.at[3], recv.at[3])
    ones = jnp.ones((16, 128), BF16)

    def receive(half, part):
        start = pl.multiple_of(half * 512 + part * 256, 256)
        at = pl.ds(start, 256)
        wide = unpack(ref.land_p[half, part * 32 : part * 32 + 32])
        empty = wide > 0.5 * EMPTY
        real = jnp.where(empty, 0.0, wide)
        ref.rows[at, :] = real.astype(BF16)
        count = dot(ones, jnp.where(empty[:, :128], 1.0, 0.0).astype(BF16), NT)
        first_row = lax.broadcasted_iota(jnp.int32, (16, 256), 0) == 0
        ref.bias[:, at] = jnp.where(first_row & (count > 0.5), MASKED, 0.0).astype(BF16)
        normed = normalize(real)[0].astype(BF16)
        ref.normed[at, :] = normed
        for j in range(3):
            projected = dot(ref.weight[j], normed, ((0,), (1,))).astype(BF16)
            ref.qkv[j, :, :, at] = projected.reshape(HEADS, HEAD_DIM, 256)

    for load in ref.loads[3:]:
        load.wait()
    pair_arrived(landed(core, 0), recv.at[0])
    swaps[0].start()
    receive(core, 0)
    pair_sends(me, core, ref.out_c, ref.land_c, send.at[1], (recv.at[1],))
    pair_arrived(landed(core, 1), recv.at[6])
    swaps[1].start()
    receive(core, 1)
    for part in range(2):
        pair_arrived(landed(1 - core, part), recv.at[2 + 5 * part])
        receive(1 - core, part)
    mask = ref.bias[...]

    def pair(i, carry):
        @pl.when(i == 3)
        def _():
            pair_arrived(ref.land_c.at[core], recv.at[1])
            swap_c.start()

        for u in range(4):
            h = 4 * i + u
            result, lse = forward_head(ref.qkv[0, h], ref.qkv[1, h], ref.qkv[2, h], mask)
            ref.attended[h] = result
            ref.lse[h] = jnp.broadcast_to(lse, (8, PATCH))
        return carry

    lax.fori_loop(0, HEADS // 4, pair, 0)

    def upstream_arrived():
        pair_arrived(ref.land_c.at[1 - core], recv.at[3])
        for half in range(2):
            for part in range(2):
                at = half * 512 + part * 256
                pieces = ref.land_c[half, part * 32 : part * 32 + 32]
                ref.upstream[at : at + 256, :] = unpack(pieces).astype(BF16)
        ref.permuted[...] = dot(ref.upstream[...], ref.order_b[...], NN).astype(BF16)

    def finish():
        for swap in (*swaps, swap_c):
            swap.wait_send()
        pair_sent(core, ref.out_p, send.at[0])
        pair_sent(core, ref.out_c, send.at[1])

    return slot, upstream_arrived, finish


def backward_head(query, key, value, bias, attended, upstream, lse):
    shape = (16, PATCH)
    row = lax.broadcasted_iota(jnp.int32, shape, 0)
    one = jnp.ones(shape, BF16)
    zero = jnp.zeros(shape, BF16)

    def stacked(*given):
        total = zero
        for at, value_at in enumerate(given):
            total = jnp.where(row == at, value_at, total)
        return total

    lse_pieces = split3(-jnp.broadcast_to(lse, shape))
    scaled = split3(query.astype(F32) * EXP2_SCALE)
    wide_query = jnp.concatenate([*scaled, stacked(one, *lse_pieces)], axis=0)
    wide_key = jnp.concatenate([key, key, key, stacked(bias, one, one, one)], axis=0)
    scale = HEAD_DIM**-0.5
    upstream_wide = upstream.astype(F32)
    delta = -scale * jnp.sum(upstream_wide * attended.astype(F32), axis=0, keepdims=True)
    delta_pieces = split3(jnp.broadcast_to(delta, shape))
    wide_upstream = jnp.concatenate(
        [(scale * upstream_wide).astype(BF16), stacked(*delta_pieces)], axis=0
    )
    wide_value = jnp.concatenate([value, stacked(one, one, one)], axis=0)
    d_query, d_key, d_value = [], None, None
    for part in range(2):
        at = slice(part * 512, part * 512 + 512)
        weights = jnp.exp2(dot(wide_query[:, at], wide_key, TN))
        d_scores = (weights * dot(wide_upstream[:, at], wide_value, TN)).astype(BF16)
        d_query.append(dot(key, d_scores, NT))
        more_key = dot(query[:, at], d_scores, NN)
        more_value = dot(upstream[:, at], weights.astype(BF16), NN)
        d_key = more_key if d_key is None else d_key + more_key
        d_value = more_value if d_value is None else d_value + more_value
    return jnp.concatenate(d_query, axis=1).astype(BF16), d_key.astype(BF16), d_value.astype(BF16)


def gelu_both(values):
    squared = values * values
    tangent = jnp.tanh(GELU_C * (values + 0.044715 * squared * values))
    half = 0.5 * (1.0 + tangent)
    derivative = half + 0.5 * values * (1.0 - tangent * tangent) * GELU_C * (
        1.0 + 3.0 * 0.044715 * squared
    )
    return values * half, derivative


CHUNK = 512


def row_order(to_yzx, sizes):
    place = lax.broadcasted_iota(jnp.int32, (D, D), 1)
    rest, parts = place >> 2, []
    for size in reversed(sizes):
        parts.insert(0, rest & (size - 1))
        rest = rest >> (size.bit_length() - 1)
    y, z, x = to_yzx(*parts)
    channel = (z << 6) + (x << 4) + (y << 2) + (place & 3)
    return (lax.broadcasted_iota(jnp.int32, (D, D), 0) == channel).astype(BF16)


def feed_forward(me, core, ref, upstream_arrived, part_a, part_b):
    sibling = (me, 1 - core)
    chunks = PATCH // CHUNK
    half = chunks // 2
    proj, fc1, fc2 = ref.proj, ref.fc1, ref.fc2

    def place(i):
        return lax.rem(i + half * (1 - core), chunks)

    def span(k):
        return pl.ds(pl.multiple_of(k * CHUNK, CHUNK), CHUNK)

    def copy(kind, i, src, dst):
        return pltpu.make_async_remote_copy(
            src_ref=src,
            dst_ref=dst,
            send_sem=ref.core_send.at[kind, i],
            recv_sem=ref.core_recv.at[kind, i],
            device_id=sibling,
            device_id_type=MESH,
        )

    def copy1(k):
        return copy(0, k, ref.snd1.at[span(k), :], ref.rcv1.at[span(k), :])

    def copy2(i):
        at = pl.ds(i * CHUNK, CHUNK)
        return copy(1, i, ref.snd2.at[at, :], ref.rcv2.at[at, :])

    def copy3(k):
        return copy(2, k, ref.snd3.at[span(k), :], ref.rcv3.at[span(k), :])

    for i in range(chunks):
        k = place(i)
        heads = ref.attended[:, :, span(k)].reshape(256, CHUNK)
        ref.snd1[span(k), :] = dot(heads, proj[...], TN).astype(BF16)
        copy1(k).start()
    upstream_arrived()

    for i in range(chunks):
        k = place(i)
        at = span(k)
        copy1(k).wait_recv()
        added = ref.snd1[at, :].astype(F32) + ref.rcv1[at, :].astype(F32)
        total = ref.rows[at, :].astype(F32) + added
        ref.mixed[at, :] = total
        normed, inv = normalize(total)
        ref.inverse[at, :] = jnp.broadcast_to(inv, (CHUNK, 128))
        low = normed.astype(BF16)
        ref.normed_mid[at, :] = low
        activation, derivative = gelu_both(dot(low, fc1[...], NN))
        act_low = activation.astype(BF16)
        ref.act[at, :] = act_low
        partial = dot(act_low, fc2[...], NN).astype(BF16)
        if i < half:
            ref.snd2[i * CHUNK : (i + 1) * CHUNK, :] = partial
            copy2(i).start()
        else:
            ref.own2[(i - half) * CHUNK : (i - half + 1) * CHUNK, :] = partial
        d_low = (dot(ref.upstream[at, :], fc2[...], NT) * derivative).astype(BF16)
        ref.d_pre[at, :] = d_low
        ref.snd3[at, :] = dot(d_low, fc1[...], NT).astype(BF16)
        copy3(k).start()

    for part in range(4):
        cols = slice(part * 256, part * 256 + 256)
        grad = dot(ref.permuted[...], ref.act[:, cols], TN).astype(BF16)
        ref.grad_b[:, :, :, cols] = grad.reshape(NY, NZ, 16, 256)
    part_b.start()
    for part in range(4):
        cols = slice(part * 256, part * 256 + 256)
        grad = dot(ref.normed_mid[...], ref.d_pre[:, cols], TN).astype(BF16)
        ref.grad_a[:, :, :, cols] = grad.reshape(NZ, NX, 16, 256)

    for i in range(chunks):
        k = place(i)
        at = span(k)
        copy3(k).wait_recv()
        back = ref.snd3[at, :].astype(F32) + ref.rcv3[at, :].astype(F32)
        inv = ref.inverse[at, :][:, 0:1]
        total = ref.mixed[at, :]
        center = total - jnp.mean(total, axis=-1, keepdims=True)
        normed = center * inv
        mean_grad = jnp.mean(back, axis=-1, keepdims=True)
        mean_mixed = jnp.mean(back * normed, axis=-1, keepdims=True)
        through = inv * (back - mean_grad - normed * mean_mixed)
        low = (ref.upstream[at, :].astype(F32) + through).astype(BF16)
        ref.d_mixed[at, :] = low
        heads = dot(proj[...], low, NT).astype(BF16)
        ref.d_attended[:, :, at] = heads.reshape(HEADS, HEAD_DIM, CHUNK)

    grad = dot(ref.attended[...].reshape(256, PATCH), ref.d_mixed[...], NN).T.astype(BF16)
    ref.grad_a[:, :, :, FF:AW] = grad.reshape(NZ, NX, 16, AW - FF)
    part_a.start()

    for i in range(half):
        copy2(i).wait_recv()
        own = slice(i * CHUNK, (i + 1) * CHUNK)
        added = ref.own2[own, :].astype(F32) + ref.rcv2[own, :].astype(F32)
        total = ref.mixed[span(place(i + half)), :] + added
        ref.block[i * CHUNK // 8 : (i + 1) * CHUNK // 8] = pack(total.astype(BF16).astype(F32))

    def finish():
        for k in range(chunks):
            copy1(k).wait_send()
            copy3(k).wait_send()
        for i in range(half):
            copy2(i).wait_send()

    return finish


class ReduceScatter:
    def __init__(self, me, core, x_first, grad, scratch):
        z, x, y = lax.div(me, NX * NY), lax.rem(lax.div(me, NY), NX), lax.rem(me, NY)
        at_x = [(z * NX + lax.rem(x + d, NX)) * NY + y for d in range(NX)]
        at_z = [(lax.rem(z + d, NZ) * NX + x) * NY + y for d in range(NZ)]
        at_y = [(z * NX + x) * NY + lax.rem(y + d, NY) for d in range(NY)]
        self.core, self.x_first = core, x_first
        self.peers = (at_x, at_z, at_y) if x_first else (at_y, at_z, at_x)
        self.place = (x, z, y) if x_first else (y, z, x)
        self.grad = grad
        self.land_0, self.mid, self.land_1, self.low, self.land_2, self.send, self.recv = scratch

    def copy(self, phase, d, src, dst):
        base = (0, NX - 1, NX + NZ - 2)[phase]
        return pltpu.make_async_remote_copy(
            src_ref=src,
            dst_ref=dst,
            send_sem=self.send.at[base + d - 1],
            recv_sem=self.recv.at[base + d - 1],
            device_id=(self.peers[phase][d], self.core),
            device_id_type=MESH,
        )

    def piece(self, d):
        at = lax.rem(self.place[0] + d, NX)
        return self.grad.at[:, at] if self.x_first else self.grad.at[at]

    def copies(self, phase):
        if phase == 0:
            return [self.copy(0, d, self.piece(d), self.land_0.at[d - 1]) for d in range(1, NX)]
        if phase == 1:
            z = self.place[1]
            return [
                self.copy(1, d, self.mid.at[lax.rem(z + d, NZ)], self.land_1.at[d - 1])
                for d in range(1, NZ)
            ]
        return [self.copy(2, d, self.low, self.land_2.at[d - 1]) for d in range(1, NY)]

    def start(self, phase=0):
        for one in self.copies(phase):
            one.start()

    def arrived(self, phase):
        for one in self.copies(phase):
            one.wait_recv()

    def second(self):
        self.arrived(0)
        mine = self.place[0]

        def step(i, carry):
            own = self.grad[i, mine] if self.x_first else self.grad[mine, i]
            total = own.astype(F32)
            for d in range(NX - 1):
                total = total + self.land_0[d, i].astype(F32)
            self.mid[i] = total.astype(BF16)
            return carry

        lax.fori_loop(0, NZ, step, 0)
        self.start(1)

    def third(self):
        self.arrived(1)
        total = self.mid[self.place[1]].astype(F32)
        for d in range(NZ - 1):
            total = total + self.land_1[d].astype(F32)
        self.low[...] = total.astype(BF16)
        self.start(2)

    def result(self):
        self.arrived(2)
        total = self.low[...].astype(F32)
        for d in range(NY - 1):
            total = total + self.land_2[d].astype(F32)
        result = total[0:4]
        for other in range(1, NY):
            part = total[4 * other : 4 * other + 4]
            result = jnp.where(self.place[2] == other, part, result)
        return result

    def finish(self):
        for phase in range(3):
            for one in self.copies(phase):
                one.wait_send()


class PlaneReduceScatter:
    def __init__(self, me, core, grad, scratch):
        z, x, y = lax.div(me, NX * NY), lax.rem(lax.div(me, NY), NX), lax.rem(me, NY)
        self.core, self.grad, self.place = core, grad, (z, x, y)
        self.land_0, self.mid, self.land_1, self.send, self.recv = scratch
        at = [(lax.rem(x + d // NY, NX), lax.rem(y + d % NY, NY)) for d in range(NX * NY)]
        self.plane = [((z * NX + x2) * NY + y2, x2, y2) for x2, y2 in at]
        other_z = [lax.rem(z + d, NZ) for d in range(NZ)]
        self.line = [((z2 * NX + x) * NY + y, z2) for z2 in other_z]

    def copy(self, k, src, dst, peer):
        return pltpu.make_async_remote_copy(
            src_ref=src,
            dst_ref=dst,
            send_sem=self.send.at[k],
            recv_sem=self.recv.at[k],
            device_id=(peer, self.core),
            device_id_type=MESH,
        )

    def group(self, z):
        return pl.ds(pl.multiple_of(lax.div(z, 4) * 16, 16), 16)

    def copies(self, phase):
        if phase == 0:
            return [
                self.copy(d - 1, self.grad.at[x, y], self.land_0.at[d - 1], peer)
                for d, (peer, x, y) in enumerate(self.plane)
                if d
            ]
        base = NX * NY - 2
        return [
            self.copy(base + d, self.mid.at[self.group(z), :], self.land_1.at[d - 1], peer)
            for d, (peer, z) in enumerate(self.line)
            if d
        ]

    def start(self):
        for one in self.copies(0):
            one.start()

    def second(self):
        for one in self.copies(0):
            one.wait_recv()
        _, x, y = self.place
        total = self.grad[x, y].astype(F32)
        for d in range(NX * NY - 1):
            total = total + self.land_0[d].astype(F32)
        self.mid[...] = total.astype(BF16)
        for one in self.copies(1):
            one.start()

    def result(self):
        for one in self.copies(1):
            one.wait_recv()
        z = self.place[0]
        total = self.mid[self.group(z), :].astype(F32)
        for d in range(NZ - 1):
            total = total + self.land_1[d].astype(F32)
        result = total[0:4]
        for other in range(1, 4):
            part = total[4 * other : 4 * other + 4]
            result = jnp.where(lax.rem(z, 4) == other, part, result)
        return result

    def finish(self):
        for phase in range(2):
            for one in self.copies(phase):
                one.wait_send()


def plane_scratch(columns):
    return [
        pltpu.VMEM((NX * NY - 1, 32, columns), BF16),
        pltpu.VMEM((32, columns), BF16),
        pltpu.VMEM((NZ - 1, 16, columns), BF16),
        pltpu.SemaphoreType.DMA((NX * NY + NZ - 2,)),
        pltpu.SemaphoreType.DMA((NX * NY + NZ - 2,)),
    ]


def reduce_scratch(columns):
    return [
        pltpu.VMEM((NX - 1, NZ, 16, columns), BF16),
        pltpu.VMEM((NZ, 16, columns), BF16),
        pltpu.VMEM((NZ - 1, 16, columns), BF16),
        pltpu.VMEM((16, columns), BF16),
        pltpu.VMEM((NY - 1, 16, columns), BF16),
        pltpu.SemaphoreType.DMA((NX + NY + NZ - 3,)),
        pltpu.SemaphoreType.DMA((NX + NY + NZ - 3,)),
    ]


SCRATCH = dict(
    out_p=((PAIRS, 16, D // 2), BF16),
    out_c=((PAIRS, 16, D // 2), BF16),
    land_p=((2, PAIRS, 16, D // 2), BF16),
    land_c=((2, PAIRS, 16, D // 2), BF16),
    rows=((PATCH, D), BF16),
    upstream=((PATCH, D), BF16),
    bias=((16, PATCH), BF16),
    normed=((PATCH, D), BF16),
    qkv=((3, HEADS, HEAD_DIM, PATCH), BF16),
    attended=((HEADS, HEAD_DIM, PATCH), BF16),
    lse=((HEADS, 8, PATCH), F32),
    snd1=((PATCH, D), BF16),
    rcv1=((PATCH, D), BF16),
    snd2=((PATCH // 2, D), BF16),
    rcv2=((PATCH // 2, D), BF16),
    own2=((PATCH // 2, D), BF16),
    snd3=((PATCH, D), BF16),
    rcv3=((PATCH, D), BF16),
    mixed=((PATCH, D), F32),
    normed_mid=((PATCH, D), BF16),
    inverse=((PATCH, 128), F32),
    act=((PATCH, FF), BF16),
    d_pre=((PATCH, FF), BF16),
    d_mixed=((PATCH, D), BF16),
    permuted=((PATCH, D), BF16),
    d_attended=((HEADS, HEAD_DIM, PATCH), BF16),
    block=((PAIRS, 16, D // 2), BF16),
    d_qkv=((3, HEADS, HEAD_DIM, PATCH), BF16),
    grad_a=((NZ, NX, 16, AW), BF16),
    grad_b=((NY, NZ, 16, BW), BF16),
    grad_qa=((NZ, NX, 16, QA), BF16),
    grad_qb=((NX, NY, 32, QB), BF16),
    land=((2, PAIRS, 16, D // 2), BF16),
    patch=((1, ROWS), jnp.int32),
    points=((ROWS, D), BF16),
    cotangent=((ROWS, D), BF16),
    weight=((3, D, 256), BF16),
    proj=((256, D), BF16),
    fc1=((D, FF), BF16),
    fc2=((FF, D), BF16),
    order_b=((D, D), BF16),
    order_q=((D, D), BF16),
)
SEMAPHORES = dict(near=(7,), pair_send=(7,), pair_recv=(8,), core_send=(3, 4), core_recv=(3, 4))
LOADED = ("patch", "points", "cotangent", "weight", "proj", "fc1", "fc2")
INPUTS = tuple("far_" + name for name in LOADED)
OUTPUTS = ("rows_out", "sums_a", "sums_b", "sums_qa", "sums_qb")


def block_kernel(*refs):
    names = (*INPUTS, *OUTPUTS, *SCRATCH, *SEMAPHORES)
    ref = types.SimpleNamespace(**dict(zip(names, refs)))
    rest = refs[len(names) :]
    ref.loads = [
        pltpu.make_async_copy(getattr(ref, "far_" + name), getattr(ref, name), ref.near.at[k])
        for k, name in enumerate(LOADED)
    ]
    me, core = lax.axis_index("dp"), lax.axis_index("mp")
    parts = [
        ReduceScatter(me, core, first, grad, rest[7 * i : 7 * i + 7])
        for i, (first, grad) in enumerate(
            ((True, ref.grad_a), (False, ref.grad_b), (True, ref.grad_qa))
        )
    ]
    part_qb = PlaneReduceScatter(me, core, ref.grad_qb, rest[21:])
    part_a, part_b, part_qa = parts
    others = [peer for peer, *_ in (*part_qb.plane[1:], *part_qb.line[1:])]
    slot, upstream_arrived, finish_attend = dispatch_and_attend(me, core, ref, others)
    finish_feed = feed_forward(me, core, ref, upstream_arrived, part_a, part_b)
    land, block, d_qkv = ref.land, ref.block, ref.d_qkv
    send, recv = ref.pair_send, ref.pair_recv
    pair_sends(me, core, block, land, send.at[4], (recv.at[4],), back=True)
    swap = to_sibling(me, core, land.at[core], send.at[5], recv.at[5])
    finish_attend()
    mask = ref.bias[...]

    def project(first, last):
        rows = (last - first) * HEAD_DIM
        heads = [d_qkv[j, first:last].reshape(rows, PATCH) for j in range(3)]
        return dot(jnp.concatenate(heads, axis=0), ref.normed[...], NN)

    def pair(i, carry):
        @pl.when(i == SECOND)
        def _():
            part_a.second()
            part_b.second()

        @pl.when(i == FIRST_HEADS // 2)
        def _():
            grad = project(0, FIRST_HEADS).T.astype(BF16)
            ref.grad_qa[...] = grad.reshape(NZ, NX, 16, QA)
            part_qa.start()
            pair_arrived(land.at[core], recv.at[4])
            swap.start()

        for u in range(2):
            h = 2 * i + u
            d_query, d_key, d_value = backward_head(
                ref.qkv[0, h], ref.qkv[1, h], ref.qkv[2, h], mask,
                ref.attended[h], ref.d_attended[h], ref.lse[h][0:1],
            )
            d_qkv[0, h] = d_query
            d_qkv[1, h] = d_key
            d_qkv[2, h] = d_value
        return carry

    lax.fori_loop(0, HEADS // 2, pair, 0)
    grad = dot(project(FIRST_HEADS, HEADS).astype(BF16), ref.order_q[...], NN)
    ref.grad_qb[...] = grad.T.astype(BF16).reshape(NX, NY, 32, QB)
    part_qb.start()
    part_a.third()
    part_b.third()
    part_qa.second()
    part_qb.second()
    part_qa.third()
    pair_arrived(land.at[1 - core], recv.at[5])
    total = None
    for half in range(2):
        place = lax.broadcasted_iota(jnp.int32, (PATCH // 2, ROWS), 0) + half * (PATCH // 2)
        chosen = (place == slot).astype(BF16)
        part = dot(chosen, unpack(land[half]).astype(BF16), TN)
        total = part if total is None else total + part
    ref.rows_out[...] = total.astype(BF16)
    ref.sums_a[...] = part_a.result()
    ref.sums_b[...] = part_b.result()
    swap.wait_send()
    pair_sent(core, block, send.at[4])
    finish_feed()
    ref.sums_qa[...] = part_qa.result()
    ref.sums_qb[...] = part_qb.result()
    for part in (*parts, part_qb):
        part.finish()


def whole_block(*given):
    return pl.pallas_call(
        block_kernel,
        out_shape=(
            jax.ShapeDtypeStruct((ROWS, D), BF16),
            jax.ShapeDtypeStruct((4, AW), F32),
            jax.ShapeDtypeStruct((4, BW), F32),
            jax.ShapeDtypeStruct((4, QA), F32),
            jax.ShapeDtypeStruct((4, QB), F32),
        ),
        in_specs=[pl.BlockSpec(memory_space=pl.ANY)] * len(INPUTS),
        out_specs=(VMEM,) * len(OUTPUTS),
        scratch_shapes=[
            *(pltpu.VMEM(*shape) for shape in SCRATCH.values()),
            *(pltpu.SemaphoreType.DMA(shape) for shape in SEMAPHORES.values()),
            *reduce_scratch(AW),
            *reduce_scratch(BW),
            *reduce_scratch(QA),
            *plane_scratch(QB),
        ],
        compiler_params=params(collective_id=1, has_side_effects=True),
        name="block",
    )(*given)


def finish_kernel(
    rows, sums_a, sums_b, sums_qa, sums_qb, rows_out, qkv_out, proj_out, fc1_out, fc2_out
):
    rows_out[...] = rows[...]
    fc1_out[...] = sums_a[:, :FF]
    proj_out[...] = sums_a[:, FF:]
    fc2_out[...] = sums_b[...]
    first, last = sums_qa[...], sums_qb[...]
    n, m = QA // 3, QB // 3
    for j in range(3):
        qkv_out[j, :, :n] = first[:, j * n : (j + 1) * n]
        qkv_out[j, :, n:] = last[:, j * m : (j + 1) * m]


def finish(*given):
    return pl.pallas_call(
        finish_kernel,
        out_shape=(
            jax.ShapeDtypeStruct((ROWS, D), BF16),
            jax.ShapeDtypeStruct((3, 4, 256), F32),
            jax.ShapeDtypeStruct((4, 256), F32),
            jax.ShapeDtypeStruct((4, FF), F32),
            jax.ShapeDtypeStruct((4, FF), F32),
        ),
        in_specs=[VMEM] * 5,
        out_specs=(VMEM,) * 5,
        compiler_params=params(),
        name="finish",
    )(*given)


def per_device(points, patch_of, qkv_weight, proj_weight, fc1_weight, fc2_weight, cotangent):
    landed = whole_block(
        patch_of.reshape(1, ROWS),
        points,
        cotangent,
        qkv_weight.transpose(1, 0, 2),
        proj_weight,
        fc1_weight,
        fc2_weight,
    )
    block_out, grad_qkv, grad_proj, grad_fc1, grad_fc2 = finish(*landed)
    return block_out, grad_qkv.transpose(1, 0, 2), grad_proj.T, grad_fc1, grad_fc2.T


def solution(mesh):
    placed = (
        P("dp", None),
        P("dp", None),
        P(None, None, "mp"),
        P("mp", None),
        P(None, "mp"),
        P("mp", None),
        P("dp", None),
    )
    return jax.shard_map(
        per_device,
        mesh=mesh,
        in_specs=placed,
        out_specs=(P("dp", None), P("dp", None, "mp"), P("mp", "dp"), P("dp", "mp"), P("mp", "dp")),
        check_vma=False,
    )
```
